32 devices in a mesh: gx: 8 (over z, y), gy: 4 (over x, core).
Axes of the slice: x: 2, y: 2, z: 4, core: 2. Of those that a mesh axis runs over, the one named last changes fastest.
Arguments:
- snapshot_panel: float32 [64, 65536], P(None, ('gx', 'gy')), may hold values from -2500 to 2500, as said below
- following: float32 [960, 65536], P(None, ('gx', 'gy')), may hold values from -2500 to 2500, as said below
Outputs:
- basis_rows: float32 [64, 65536], P(None, ('gx', 'gy'))
- upper_factor: float32 [64, 64], replicated
- projection: float32 [64, 960], replicated
The draws below stay inside these ranges and needn't reach their ends.
Inputs may be any that keep to these rules, and one draw needn't show every extreme that they name: `snapshot_panel`: real-valued snapshots of full rank. `following`: real-valued snapshots.
All inputs are finite; a program needn't handle non-finite values.
Results may differ from the reference program's by a relative error of at most 0.000077.
Values sent between devices are 32-bit elements; how exact they have to be, the bound alone decides.
A program may use at most 64 MiB of HBM per device.

```python
import math
import jax
import jax.numpy as jnp
from jax import lax

P_SIZE = 64
NEXT = 960
ROWS = 65536


def common_parts(key, spread_log):
    keys = jax.random.split(key, 4)
    normal_part = jax.random.truncated_normal(keys[0], -4.0, 4.0, (P_SIZE, ROWS), jnp.float32)
    position = jnp.arange(ROWS, dtype=jnp.float32) / ROWS
    row_scale = (1.0 + 2.0 * position) * jnp.exp(jax.random.uniform(keys[2], (ROWS,), jnp.float32) * spread_log)
    col_scale = jnp.exp(jax.random.uniform(keys[3], (P_SIZE, 1), jnp.float32) * math.log(10.0))
    return (normal_part * col_scale, row_scale[None, :])


def draw_snapshot_panel(key, part):
    columns, row_scale = common_parts(key, math.log(3.0))
    return (columns * row_scale).astype(jnp.float32)


def draw_following(key, part):
    columns, row_scale = common_parts(key, math.log(3.0))
    own_key = jax.random.fold_in(key, 7)
    noise_key, scale_key = jax.random.split(own_key, 2)
    noise = jax.random.truncated_normal(noise_key, -4.0, 4.0, (NEXT, ROWS), jnp.float32)
    noise_scale = jnp.exp(jax.random.uniform(scale_key, (NEXT, 1), jnp.float32) * math.log(10.0))
    repeated = jnp.tile(columns, (NEXT // P_SIZE, 1))
    return (row_scale * (0.6 * repeated + noise * noise_scale)).astype(jnp.float32)


def setup_inputs(seed: int = 0) -> dict:
    arg_keys = jax.random.split(jax.random.key(seed), 3)
    snapshot_panel = draw_snapshot_panel(jax.random.fold_in(arg_keys[2], 71), 0)
    following = draw_following(jax.random.fold_in(arg_keys[2], 71), 0)
    return dict(snapshot_panel=snapshot_panel, following=following)


def inner_product(left, right):
    return lax.dot_general(left.astype(jnp.float32), right.astype(jnp.float32), (((1,), (1,)), ((), ())), precision=lax.Precision.HIGHEST, preferred_element_type=jnp.float32)

def reference(snapshot_panel, following):
    gram_matrix = inner_product(snapshot_panel, snapshot_panel)
    lower_factor = jnp.linalg.cholesky(gram_matrix)
    cross_terms = inner_product(snapshot_panel, following)
    root_rows = math.sqrt(ROWS)
    basis_rows = jax.scipy.linalg.solve_triangular(lower_factor, snapshot_panel, lower=True) * root_rows
    upper_factor = lower_factor.T / root_rows
    projection = jax.scipy.linalg.solve_triangular(lower_factor, cross_terms, lower=True) / root_rows
    return (basis_rows, upper_factor, projection)
```

```python
import math

import jax
import jax.numpy as jnp
from jax import lax
from jax.sharding import PartitionSpec as P


def inner_product(left, right):
    return lax.dot_general(
        left,
        right,
        (((1,), (1,)), ((), ())),
        precision=lax.Precision.HIGHEST,
        preferred_element_type=jnp.float32,
    )


def lower_solve(lower_factor, values):
    return jax.scipy.linalg.solve_triangular(lower_factor, values, lower=True)


def body(snapshot_panel, following):
    panel_width = snapshot_panel.shape[0]
    root_rows = math.sqrt(snapshot_panel.shape[1] * lax.axis_size(("gx", "gy")))
    local = jnp.concatenate(
        [inner_product(snapshot_panel, snapshot_panel), inner_product(snapshot_panel, following)],
        axis=1,
    )
    summed = lax.psum(local, ("gx", "gy"))
    lower_factor = jnp.linalg.cholesky(summed[:, :panel_width])
    projected = lower_solve(lower_factor, summed[:, panel_width:])
    basis_local = lower_solve(lower_factor, snapshot_panel)
    return (basis_local * root_rows, lower_factor.T / root_rows, projected / root_rows)


def solution(mesh):
    return jax.shard_map(
        body,
        mesh=mesh,
        in_specs=(P(None, ("gx", "gy")), P(None, ("gx", "gy"))),
        out_specs=(P(None, ("gx", "gy")), P(), P()),
        check_vma=False,
    )
```

```python
import functools
import math

import jax
import jax.numpy as jnp
from jax import lax
from jax.experimental import pallas as pl
from jax.experimental.pallas import tpu as pltpu
from jax.sharding import PartitionSpec as P

MESH = pl.DeviceIdType.MESH
LANES = 128


def halves(values):
    high = values.astype(jnp.bfloat16)
    return high, (values - high.astype(jnp.float32)).astype(jnp.bfloat16)


def rows_product(left, right):
    return lax.dot_general(
        left, right, (((1,), (1,)), ((), ())), preferred_element_type=jnp.float32
    )


def ordered_sum(own_ref, slots_ref, me, count):
    result = jnp.zeros(own_ref.shape, own_ref.dtype)
    for source in range(count):
        back = lax.rem(me - source + count, count)
        taken = slots_ref[lax.max(back - 1, 0)]
        result = result + jnp.where(back == 0, own_ref[...], taken)
    return result


def sum_kernel(
    n_gx,
    n_gy,
    panel_ref,
    following_ref,
    sums_ref,
    gram_ref,
    panel_vmem,
    rows_vmem,
    panel_split,
    part,
    gram_own,
    gram_gy,
    gram_mid,
    gram_gx,
    half_in,
    half_sum,
    piece_in,
    total,
    load_panel_sem,
    load_sem,
    gy_send,
    gy_recv,
    gx_send,
    gx_recv,
    half_send,
    half_recv,
    rs_send,
    rs_recv,
    ag_send,
    ag_recv,
    back_send,
    back_recv,
):
    width = panel_ref.shape[0]
    units = rows_vmem.shape[0] // width
    blocks = rows_vmem.shape[0] // LANES
    half_blocks = blocks // 2
    half_rows = half_blocks * width
    n_chips = n_gx * n_gy // 2
    piece = half_rows // n_chips
    me_x, me_y = lax.axis_index("gx"), lax.axis_index("gy")
    core = lax.rem(me_y, 2)
    other = 1 - core
    chip = me_x * (n_gy // 2) + me_y // 2
    sibling = (me_x, me_y + 1 - 2 * core)

    def chip_device(index):
        return (index // (n_gy // 2), lax.rem(index, n_gy // 2) * 2 + core)

    load_panel = pltpu.make_async_copy(panel_ref, panel_vmem, load_panel_sem)
    load_panel.start()

    def load(source, unit):
        pltpu.make_async_copy(
            source, rows_vmem.at[pl.ds(unit * width, width)], load_sem.at[unit]
        ).start()

    for step in range(units):
        unit = lax.rem(step + other * (units // 2), units)
        if step % (units // 2) != units // 2 - 1:
            load(following_ref.at[pl.ds(unit * width, width)], unit)
        else:
            @pl.when(unit == units - 1)
            def _():
                load(panel_ref, unit)

            @pl.when(unit != units - 1)
            def _():
                load(following_ref.at[pl.ds(unit * width, width)], unit)

    barrier = pltpu.get_barrier_semaphore()
    n_signals = 0
    for k in range(1, n_chips):
        pl.semaphore_signal(
            barrier, inc=1, device_id=chip_device(lax.rem(chip + k, n_chips)), device_id_type=MESH
        )
        n_signals += 1
    for k in range(1, n_gy, 2):
        pl.semaphore_signal(
            barrier, inc=1, device_id=(me_x, lax.rem(me_y + k, n_gy)), device_id_type=MESH
        )
        n_signals += 1

    load_panel.wait()
    high, low = halves(panel_vmem[...])
    panel_split[0:width, :] = high
    panel_split[width : 2 * width, :] = low
    quads = rows_product(panel_split[...], panel_split[...])
    pair = quads[:width] + quads[width:]
    gram = pair[:, :width] + pair[:, width:]
    gram_own[...] = jnp.concatenate([gram[: width // 2], gram[width // 2 :]], axis=1)

    pl.semaphore_wait(barrier, n_signals)

    gy_copies = []
    for k in range(1, n_gy):
        copy = pltpu.make_async_remote_copy(
            src_ref=gram_own,
            dst_ref=gram_gy.at[k - 1],
            send_sem=gy_send.at[k - 1],
            recv_sem=gy_recv.at[k - 1],
            device_id=(me_x, lax.rem(me_y + k, n_gy)),
            device_id_type=MESH,
        )
        copy.start()
        gy_copies.append(copy)

    def cross(block):
        for unit in (2 * block, 2 * block + 1):
            pltpu.make_async_copy(
                panel_ref, rows_vmem.at[pl.ds(unit * width, width)], load_sem.at[unit]
            ).wait()
        row_high, row_low = halves(rows_vmem[pl.ds(block * LANES, LANES), :])
        split = panel_split[...]
        turned = (rows_product(row_high, split) + rows_product(row_low, split)).T
        part[pl.ds(block * width, width), :] = turned[:width] + turned[width:]

    @pl.loop(0, half_blocks)
    def _(i):
        cross(other * half_blocks + i)

    half_copy = pltpu.make_async_remote_copy(
        src_ref=part.at[pl.ds(other * half_rows, half_rows)],
        dst_ref=half_in,
        send_sem=half_send,
        recv_sem=half_recv,
        device_id=sibling,
        device_id_type=MESH,
    )
    half_copy.start()

    for copy in gy_copies:
        copy.wait_recv()
    gram_mid[...] = ordered_sum(gram_own, gram_gy, me_y, n_gy)
    gx_copies = []
    for k in range(1, n_gx):
        copy = pltpu.make_async_remote_copy(
            src_ref=gram_mid,
            dst_ref=gram_gx.at[k - 1],
            send_sem=gx_send.at[k - 1],
            recv_sem=gx_recv.at[k - 1],
            device_id=(lax.rem(me_x + k, n_gx), me_y),
            device_id_type=MESH,
        )
        copy.start()
        gx_copies.append(copy)

    @pl.loop(0, half_blocks)
    def _(i):
        cross(core * half_blocks + i)

    half_copy.wait_recv()
    half_sum[...] = part[pl.ds(core * half_rows, half_rows), :] + half_in[...]
    rs_copies = []
    for k in range(1, n_chips):
        to = lax.rem(chip + k, n_chips)
        copy = pltpu.make_async_remote_copy(
            src_ref=half_sum.at[pl.ds(to * piece, piece)],
            dst_ref=piece_in.at[k - 1],
            send_sem=rs_send.at[k - 1],
            recv_sem=rs_recv.at[k - 1],
            device_id=chip_device(to),
            device_id_type=MESH,
        )
        copy.start()
        rs_copies.append(copy)

    for copy in gx_copies:
        copy.wait_recv()
    gram_ref[...] = ordered_sum(gram_mid, gram_gx, me_x, n_gx)

    for copy in rs_copies:
        copy.wait_recv()
    own_start = core * half_rows + chip * piece
    own = half_sum[pl.ds(chip * piece, piece), :]
    for k in range(n_chips - 1):
        own = own + piece_in[k]
    total[pl.ds(own_start, piece), :] = own

    ag_copies = []
    for k in range(1, n_chips):
        copy = pltpu.make_async_remote_copy(
            src_ref=total.at[pl.ds(own_start, piece)],
            dst_ref=total.at[pl.ds(own_start, piece)],
            send_sem=ag_send.at[k - 1],
            recv_sem=ag_recv.at[k - 1],
            device_id=chip_device(lax.rem(chip + k, n_chips)),
            device_id_type=MESH,
        )
        copy.start()
        ag_copies.append(copy)
    for copy in ag_copies:
        copy.wait_recv()
    back_copy = pltpu.make_async_remote_copy(
        src_ref=total.at[pl.ds(core * half_rows, half_rows)],
        dst_ref=total.at[pl.ds(core * half_rows, half_rows)],
        send_sem=back_send,
        recv_sem=back_recv,
        device_id=sibling,
        device_id_type=MESH,
    )
    back_copy.start()
    back_copy.wait_recv()
    sums_ref[...] = total[...]
    back_copy.wait_send()
    for copy in gy_copies + gx_copies + [half_copy] + rs_copies + ag_copies:
        copy.wait_send()


def summed_blocks(panel, following, n_gx, n_gy):
    width, cells = panel.shape
    rows = width + following.shape[0]
    all_rows = rows // LANES * width
    half_rows = all_rows // 2
    n_chips = n_gx * n_gy // 2
    piece = half_rows // n_chips
    gram_block = (width // 2, 2 * width)
    dma = pltpu.SemaphoreType.DMA
    f32 = jnp.float32
    return pl.pallas_call(
        functools.partial(sum_kernel, n_gx, n_gy),
        out_shape=(
            jax.ShapeDtypeStruct((all_rows, LANES), f32),
            jax.ShapeDtypeStruct(gram_block, f32),
        ),
        in_specs=[pl.BlockSpec(memory_space=pl.ANY)] * 2,
        out_specs=(pl.BlockSpec(memory_space=pltpu.VMEM),) * 2,
        scratch_shapes=[
            pltpu.VMEM((width, cells), f32),
            pltpu.VMEM((rows, cells), f32),
            pltpu.VMEM((2 * width, cells), jnp.bfloat16),
            pltpu.VMEM((all_rows, LANES), f32),
            pltpu.VMEM(gram_block, f32),
            pltpu.VMEM((n_gy - 1,) + gram_block, f32),
            pltpu.VMEM(gram_block, f32),
            pltpu.VMEM((n_gx - 1,) + gram_block, f32),
            pltpu.VMEM((half_rows, LANES), f32),
            pltpu.VMEM((half_rows, LANES), f32),
            pltpu.VMEM((n_chips - 1, piece, LANES), f32),
            pltpu.VMEM((all_rows, LANES), f32),
            dma,
            dma((rows // width,)),
            dma((n_gy - 1,)),
            dma((n_gy - 1,)),
            dma((n_gx - 1,)),
            dma((n_gx - 1,)),
            dma,
            dma,
            dma((n_chips - 1,)),
            dma((n_chips - 1,)),
            dma((n_chips - 1,)),
            dma((n_chips - 1,)),
            dma,
            dma,
        ],
        compiler_params=pltpu.CompilerParams(
            collective_id=0, has_side_effects=True, vmem_limit_bytes=40 * 2**20
        ),
        name="sum_blocks",
    )(panel, following)


def eliminate(gram, out_ref):
    width = gram.shape[0]
    row = lax.broadcasted_iota(jnp.int32, (width, width), 0)
    column = lax.broadcasted_iota(jnp.int32, (width, width), 1)
    wide = jnp.concatenate([gram, jnp.where(row == column, 1.0, 0.0)], axis=1)
    n_groups = width // 8
    sublane = lax.broadcasted_iota(jnp.int32, (8, 2 * width), 0)
    group = [wide[8 * g : 8 * g + 8, :] for g in range(n_groups)]
    step = 4
    for first in range(0, width, step):
        g0 = first // 8
        live = range(g0, n_groups)
        columns = [
            {
                g: jnp.broadcast_to(group[g][:, first + k : first + k + 1], (8, 2 * width))
                for g in live
            }
            for k in range(step)
        ]
        for k in range(step):
            r = (first + k) % 8
            pivot_row = group[g0][r : r + 1, :]
            pivot = columns[k][g0][r : r + 1, :]
            inverse = 1.0 / pivot
            out_ref[first + k : first + k + 1, :] = pivot_row * lax.rsqrt(pivot)
            scaled_row = pivot_row * inverse
            heads = [columns[l][g0][r : r + 1, :] * inverse for l in range(k + 1, step)]
            for g in live:
                factor = columns[k][g]
                if g == g0:
                    factor = jnp.where(sublane > r, factor, 0.0)
                group[g] = group[g] - factor * scaled_row
                for l in range(k + 1, step):
                    columns[l][g] = columns[l][g] - factor * heads[l - k - 1]


def factor_kernel(root_rows, sums_ref, gram_ref, panel_ref, basis_ref, upper_ref, proj_ref, wide_ref):
    width, cells = panel_ref.shape
    packed = gram_ref[...]
    eliminate(jnp.concatenate([packed[:, :width], packed[:, width:]], axis=0), wide_ref)
    row = lax.broadcasted_iota(jnp.int32, (width, width), 0)
    column = lax.broadcasted_iota(jnp.int32, (width, width), 1)
    wide = wide_ref[...]
    upper_ref[...] = jnp.where(column >= row, wide[:, :width], 0.0) * (1.0 / root_rows)
    high, low = halves(wide[:, width:])
    stacked = jnp.concatenate([high, high, low, low], axis=1)

    def apply(values):
        value_high, value_low = halves(values)
        return jnp.dot(
            stacked,
            jnp.concatenate([value_high, value_low, value_high, value_low], axis=0),
            preferred_element_type=jnp.float32,
        )

    for start in range(0, proj_ref.shape[1], LANES):
        count = min(LANES, proj_ref.shape[1] - start)
        first = start // LANES * width
        proj_ref[:, start : start + count] = (
            apply(sums_ref[first : first + width, :]) * (1.0 / root_rows)
        )[:, :count]
    chunk = 256
    for start in range(0, cells, chunk):
        basis_ref[:, start : start + chunk] = (
            apply(panel_ref[:, start : start + chunk]) * root_rows
        )


def factored(sums, gram, panel, next_count, root_rows):
    width, cells = panel.shape
    f32 = jnp.float32
    return pl.pallas_call(
        functools.partial(factor_kernel, root_rows),
        out_shape=(
            jax.ShapeDtypeStruct((width, cells), f32),
            jax.ShapeDtypeStruct((width, width), f32),
            jax.ShapeDtypeStruct((width, next_count), f32),
        ),
        scratch_shapes=[pltpu.VMEM((width, 2 * width), f32)],
        compiler_params=pltpu.CompilerParams(vmem_limit_bytes=16 * 2**20),
        name="factor_and_apply",
    )(sums, gram, panel)


def plain_sums(panel, following):
    precise = functools.partial(
        lax.dot_general,
        dimension_numbers=(((1,), (1,)), ((), ())),
        precision=lax.Precision.HIGHEST,
        preferred_element_type=jnp.float32,
    )
    width = panel.shape[0]
    cross = lax.psum(
        jnp.concatenate([precise(panel, following), precise(panel, panel)], axis=1), ("gx", "gy")
    )
    blocks = cross.shape[1] // LANES
    sums = cross.reshape(width, blocks, LANES).transpose(1, 0, 2).reshape(blocks * width, LANES)
    gram = cross[:, -width:]
    return sums, jnp.concatenate([gram[: width // 2], gram[width // 2 :]], axis=1)


def body(n_gx, n_gy, panel, following):
    width, cells = panel.shape
    root_rows = math.sqrt(cells * n_gx * n_gy)
    half_rows = (width + following.shape[0]) // LANES * width // 2
    if half_rows % (8 * (n_gx * n_gy // 2)) == 0:
        sums, gram = summed_blocks(panel, following, n_gx, n_gy)
    else:
        sums, gram = plain_sums(panel, following)
    return factored(sums, gram, panel, following.shape[0], root_rows)


def solution(mesh):
    return jax.shard_map(
        functools.partial(body, mesh.shape["gx"], mesh.shape["gy"]),
        mesh=mesh,
        in_specs=(P(None, ("gx", "gy")), P(None, ("gx", "gy"))),
        out_specs=(P(None, ("gx", "gy")), P(), P()),
        check_vma=False,
    )
```

```python
import functools
import math

import jax
import jax.numpy as jnp
from jax import lax
from jax.experimental import pallas as pl
from jax.experimental.pallas import tpu as pltpu
from jax.sharding import PartitionSpec as P

MESH = pl.DeviceIdType.MESH
LANES = 128


def halves(values):
    high = values.astype(jnp.bfloat16)
    return high, (values - high.astype(jnp.float32)).astype(jnp.bfloat16)


def rows_product(left, right):
    return lax.dot_general(
        left, right, (((1,), (1,)), ((), ())), preferred_element_type=jnp.float32
    )


def eliminate(gram, out_ref):
    width = gram.shape[0]
    row = lax.broadcasted_iota(jnp.int32, (width, width), 0)
    column = lax.broadcasted_iota(jnp.int32, (width, width), 1)
    wide = jnp.concatenate([gram, jnp.where(row == column, 1.0, 0.0)], axis=1)
    n_groups = width // 8
    sublane = lax.broadcasted_iota(jnp.int32, (8, 2 * width), 0)
    group = [wide[8 * g : 8 * g + 8, :] for g in range(n_groups)]
    step = 4
    for first in range(0, width, step):
        g0 = first // 8
        live = range(g0, n_groups)
        columns = [
            {
                g: jnp.broadcast_to(group[g][:, first + k : first + k + 1], (8, 2 * width))
                for g in live
            }
            for k in range(step)
        ]
        for k in range(step):
            r = (first + k) % 8
            pivot_row = group[g0][r : r + 1, :]
            pivot = columns[k][g0][r : r + 1, :]
            inverse = 1.0 / pivot
            out_ref[first + k : first + k + 1, :] = pivot_row * lax.rsqrt(pivot)
            scaled_row = pivot_row * inverse
            heads = [columns[l][g0][r : r + 1, :] * inverse for l in range(k + 1, step)]
            for g in live:
                factor = columns[k][g]
                if g == g0:
                    factor = jnp.where(sublane > r, factor, 0.0)
                group[g] = group[g] - factor * scaled_row
                for l in range(k + 1, step):
                    columns[l][g] = columns[l][g] - factor * heads[l - k - 1]


def ordered_sum(own_ref, slots_ref, me, count):
    result = jnp.zeros(own_ref.shape, own_ref.dtype)
    for source in range(count):
        back = lax.rem(me - source + count, count)
        taken = slots_ref[lax.max(back - 1, 0)]
        result = result + jnp.where(back == 0, own_ref[...], taken)
    return result


def sum_kernel(
    n_gx,
    n_gy,
    panel_ref,
    following_ref,
    sums_ref,
    wide_ref,
    panel_vmem,
    rows_vmem,
    panel_split,
    part,
    gram_own,
    gram_gy,
    gram_mid,
    gram_gx,
    half_in,
    half_sum,
    piece_in,
    total,
    load_panel_sem,
    load_sem,
    gy_send,
    gy_recv,
    gx_send,
    gx_recv,
    half_send,
    half_recv,
    rs_send,
    rs_recv,
    ag_send,
    ag_recv,
    back_send,
    back_recv,
):
    width = panel_ref.shape[0]
    units = rows_vmem.shape[0] // width
    blocks = rows_vmem.shape[0] // LANES
    half_blocks = blocks // 2
    half_rows = half_blocks * width
    n_chips = n_gx * n_gy // 2
    piece = half_rows // n_chips
    me_x, me_y = lax.axis_index("gx"), lax.axis_index("gy")
    core = lax.rem(me_y, 2)
    other = 1 - core
    chip = me_x * (n_gy // 2) + me_y // 2
    sibling = (me_x, me_y + 1 - 2 * core)

    def chip_device(index):
        return (index // (n_gy // 2), lax.rem(index, n_gy // 2) * 2 + core)

    load_panel = pltpu.make_async_copy(panel_ref, panel_vmem, load_panel_sem)
    load_panel.start()

    def load(source, unit):
        pltpu.make_async_copy(
            source, rows_vmem.at[pl.ds(unit * width, width)], load_sem.at[unit]
        ).start()

    for step in range(units):
        unit = lax.rem(step + other * (units // 2), units)
        if step % (units // 2) != units // 2 - 1:
            load(following_ref.at[pl.ds(unit * width, width)], unit)
        else:
            @pl.when(unit == units - 1)
            def _():
                load(panel_ref, unit)

            @pl.when(unit != units - 1)
            def _():
                load(following_ref.at[pl.ds(unit * width, width)], unit)

    barrier = pltpu.get_barrier_semaphore()
    n_signals = 0
    for k in range(1, n_chips):
        pl.semaphore_signal(
            barrier, inc=1, device_id=chip_device(lax.rem(chip + k, n_chips)), device_id_type=MESH
        )
        n_signals += 1
    for k in range(1, n_gy, 2):
        pl.semaphore_signal(
            barrier, inc=1, device_id=(me_x, lax.rem(me_y + k, n_gy)), device_id_type=MESH
        )
        n_signals += 1

    load_panel.wait()
    high, low = halves(panel_vmem[...])
    panel_split[0:width, :] = high
    panel_split[width : 2 * width, :] = low
    quads = rows_product(panel_split[...], panel_split[...])
    pair = quads[:width] + quads[width:]
    gram = pair[:, :width] + pair[:, width:]
    gram_own[...] = jnp.concatenate([gram[: width // 2], gram[width // 2 :]], axis=1)

    pl.semaphore_wait(barrier, n_signals)

    gy_copies = []
    for k in range(1, n_gy):
        copy = pltpu.make_async_remote_copy(
            src_ref=gram_own,
            dst_ref=gram_gy.at[k - 1],
            send_sem=gy_send.at[k - 1],
            recv_sem=gy_recv.at[k - 1],
            device_id=(me_x, lax.rem(me_y + k, n_gy)),
            device_id_type=MESH,
        )
        copy.start()
        gy_copies.append(copy)

    batch = 2 * LANES
    half_batches = half_blocks // 2

    def cross(index):
        for k in range(batch // width):
            unit = index * (batch // width) + k
            pltpu.make_async_copy(
                panel_ref, rows_vmem.at[pl.ds(unit * width, width)], load_sem.at[unit]
            ).wait()
        row_high, row_low = halves(rows_vmem[pl.ds(index * batch, batch), :])
        quads = rows_product(jnp.concatenate([row_high, row_low], axis=0), panel_split[...])
        pair = quads[:batch] + quads[batch:]
        for k in range(batch // LANES):
            turned = pair[k * LANES : (k + 1) * LANES].T
            block = index * (batch // LANES) + k
            part[pl.ds(block * width, width), :] = turned[:width] + turned[width:]

    @pl.loop(0, half_batches)
    def _(i):
        cross(other * half_batches + i)

    half_copy = pltpu.make_async_remote_copy(
        src_ref=part.at[pl.ds(other * half_rows, half_rows)],
        dst_ref=half_in,
        send_sem=half_send,
        recv_sem=half_recv,
        device_id=sibling,
        device_id_type=MESH,
    )
    half_copy.start()

    for copy in gy_copies:
        copy.wait_recv()
    gram_mid[...] = ordered_sum(gram_own, gram_gy, me_y, n_gy)
    gx_copies = []
    for k in range(1, n_gx):
        copy = pltpu.make_async_remote_copy(
            src_ref=gram_mid,
            dst_ref=gram_gx.at[k - 1],
            send_sem=gx_send.at[k - 1],
            recv_sem=gx_recv.at[k - 1],
            device_id=(lax.rem(me_x + k, n_gx), me_y),
            device_id_type=MESH,
        )
        copy.start()
        gx_copies.append(copy)

    @pl.loop(0, half_batches)
    def _(i):
        cross(core * half_batches + i)

    half_copy.wait_recv()
    half_sum[...] = part[pl.ds(core * half_rows, half_rows), :] + half_in[...]
    rs_copies = []
    for k in range(1, n_chips):
        to = lax.rem(chip + k, n_chips)
        copy = pltpu.make_async_remote_copy(
            src_ref=half_sum.at[pl.ds(to * piece, piece)],
            dst_ref=piece_in.at[k - 1],
            send_sem=rs_send.at[k - 1],
            recv_sem=rs_recv.at[k - 1],
            device_id=chip_device(to),
            device_id_type=MESH,
        )
        copy.start()
        rs_copies.append(copy)

    for copy in gx_copies:
        copy.wait_recv()
    packed = ordered_sum(gram_mid, gram_gx, me_x, n_gx)
    eliminate(jnp.concatenate([packed[:, :width], packed[:, width:]], axis=0), wide_ref)

    for copy in rs_copies:
        copy.wait_recv()
    own_start = core * half_rows + chip * piece
    own = half_sum[pl.ds(chip * piece, piece), :]
    for k in range(n_chips - 1):
        own = own + piece_in[k]
    total[pl.ds(own_start, piece), :] = own

    ag_copies = []
    for k in range(1, n_chips):
        copy = pltpu.make_async_remote_copy(
            src_ref=total.at[pl.ds(own_start, piece)],
            dst_ref=total.at[pl.ds(own_start, piece)],
            send_sem=ag_send.at[k - 1],
            recv_sem=ag_recv.at[k - 1],
            device_id=chip_device(lax.rem(chip + k, n_chips)),
            device_id_type=MESH,
        )
        copy.start()
        ag_copies.append(copy)
    for copy in ag_copies:
        copy.wait_recv()
    back_copy = pltpu.make_async_remote_copy(
        src_ref=total.at[pl.ds(core * half_rows, half_rows)],
        dst_ref=total.at[pl.ds(core * half_rows, half_rows)],
        send_sem=back_send,
        recv_sem=back_recv,
        device_id=sibling,
        device_id_type=MESH,
    )
    back_copy.start()
    back_copy.wait_recv()
    sums_ref[...] = total[...]
    back_copy.wait_send()
    for copy in gy_copies + gx_copies + [half_copy] + rs_copies + ag_copies:
        copy.wait_send()


def summed_blocks(panel, following, n_gx, n_gy):
    width, cells = panel.shape
    rows = width + following.shape[0]
    all_rows = rows // LANES * width
    half_rows = all_rows // 2
    n_chips = n_gx * n_gy // 2
    piece = half_rows // n_chips
    gram_block = (width // 2, 2 * width)
    dma = pltpu.SemaphoreType.DMA
    f32 = jnp.float32
    return pl.pallas_call(
        functools.partial(sum_kernel, n_gx, n_gy),
        out_shape=(
            jax.ShapeDtypeStruct((all_rows, LANES), f32),
            jax.ShapeDtypeStruct((width, 2 * width), f32),
        ),
        in_specs=[pl.BlockSpec(memory_space=pltpu.HBM)] * 2,
        out_specs=(pl.BlockSpec(memory_space=pltpu.VMEM),) * 2,
        scratch_shapes=[
            pltpu.VMEM((width, cells), f32),
            pltpu.VMEM((rows, cells), f32),
            pltpu.VMEM((2 * width, cells), jnp.bfloat16),
            pltpu.VMEM((all_rows, LANES), f32),
            pltpu.VMEM(gram_block, f32),
            pltpu.VMEM((n_gy - 1,) + gram_block, f32),
            pltpu.VMEM(gram_block, f32),
            pltpu.VMEM((n_gx - 1,) + gram_block, f32),
            pltpu.VMEM((half_rows, LANES), f32),
            pltpu.VMEM((half_rows, LANES), f32),
            pltpu.VMEM((n_chips - 1, piece, LANES), f32),
            pltpu.VMEM((all_rows, LANES), f32),
            dma,
            dma((rows // width,)),
            dma((n_gy - 1,)),
            dma((n_gy - 1,)),
            dma((n_gx - 1,)),
            dma((n_gx - 1,)),
            dma,
            dma,
            dma((n_chips - 1,)),
            dma((n_chips - 1,)),
            dma((n_chips - 1,)),
            dma((n_chips - 1,)),
            dma,
            dma,
        ],
        compiler_params=pltpu.CompilerParams(
            collective_id=0, has_side_effects=True, vmem_limit_bytes=56 * 2**20
        ),
        name="sum_blocks",
    )(panel, following)


def apply_kernel(root_rows, sums_ref, wide_ref, panel_ref, basis_ref, upper_ref, proj_ref):
    width, cells = panel_ref.shape
    row = lax.broadcasted_iota(jnp.int32, (width, width), 0)
    column = lax.broadcasted_iota(jnp.int32, (width, width), 1)
    wide = wide_ref[...]
    upper_ref[...] = jnp.where(column >= row, wide[:, :width], 0.0) * (1.0 / root_rows)
    high, low = halves(wide[:, width:])
    stacked = jnp.concatenate([high, high, low, low], axis=1)

    def apply(values):
        value_high, value_low = halves(values)
        return jnp.dot(
            stacked,
            jnp.concatenate([value_high, value_low, value_high, value_low], axis=0),
            preferred_element_type=jnp.float32,
        )

    for start in range(0, proj_ref.shape[1], LANES):
        count = min(LANES, proj_ref.shape[1] - start)
        first = start // LANES * width
        proj_ref[:, start : start + count] = (
            apply(sums_ref[first : first + width, :]) * (1.0 / root_rows)
        )[:, :count]
    chunk = 256
    for start in range(0, cells, chunk):
        basis_ref[:, start : start + chunk] = (
            apply(panel_ref[:, start : start + chunk]) * root_rows
        )


def applied(sums, wide, panel, next_count, root_rows):
    width, cells = panel.shape
    f32 = jnp.float32
    return pl.pallas_call(
        functools.partial(apply_kernel, root_rows),
        out_shape=(
            jax.ShapeDtypeStruct((width, cells), f32),
            jax.ShapeDtypeStruct((width, width), f32),
            jax.ShapeDtypeStruct((width, next_count), f32),
        ),
        compiler_params=pltpu.CompilerParams(vmem_limit_bytes=60 * 2**20),
        name="apply_factor",
    )(sums, wide, panel)


def plain_sums(panel, following):
    precise = functools.partial(
        lax.dot_general,
        dimension_numbers=(((1,), (1,)), ((), ())),
        precision=lax.Precision.HIGHEST,
        preferred_element_type=jnp.float32,
    )
    width = panel.shape[0]
    cross = lax.psum(
        jnp.concatenate([precise(panel, following), precise(panel, panel)], axis=1), ("gx", "gy")
    )
    blocks = cross.shape[1] // LANES
    sums = cross.reshape(width, blocks, LANES).transpose(1, 0, 2).reshape(blocks * width, LANES)
    wide = pl.pallas_call(
        lambda gram_ref, wide_ref: eliminate(gram_ref[...], wide_ref),
        out_shape=jax.ShapeDtypeStruct((width, 2 * width), jnp.float32),
        name="factor",
    )(cross[:, -width:])
    return sums, wide


def body(n_gx, n_gy, panel, following):
    width, cells = panel.shape
    root_rows = math.sqrt(cells * n_gx * n_gy)
    half_rows = (width + following.shape[0]) // LANES * width // 2
    if half_rows % (8 * (n_gx * n_gy // 2)) == 0:
        sums, wide = summed_blocks(panel, following, n_gx, n_gy)
    else:
        sums, wide = plain_sums(panel, following)
    return applied(sums, wide, panel, following.shape[0], root_rows)


def solution(mesh):
    return jax.shard_map(
        functools.partial(body, mesh.shape["gx"], mesh.shape["gy"]),
        mesh=mesh,
        in_specs=(P(None, ("gx", "gy")), P(None, ("gx", "gy"))),
        out_specs=(P(None, ("gx", "gy")), P(), P()),
        check_vma=False,
    )
```

```python
import functools
import math

import jax
import jax.numpy as jnp
from jax import lax
from jax.experimental import pallas as pl
from jax.experimental.pallas import tpu as pltpu
from jax.sharding import PartitionSpec as P

MESH = pl.DeviceIdType.MESH
LANES = 128
BATCH = 256


def halves(values):
    high = values.astype(jnp.bfloat16)
    return high, (values - high.astype(jnp.float32)).astype(jnp.bfloat16)


def rows_product(left, right):
    return lax.dot_general(
        left, right, (((1,), (1,)), ((), ())), preferred_element_type=jnp.float32
    )


def eliminate(gram, out_ref):
    width = gram.shape[0]
    row = lax.broadcasted_iota(jnp.int32, (width, width), 0)
    column = lax.broadcasted_iota(jnp.int32, (width, width), 1)
    wide = jnp.concatenate([gram, jnp.where(row == column, 1.0, 0.0)], axis=1)
    n_groups = width // 8
    sublane = lax.broadcasted_iota(jnp.int32, (8, 2 * width), 0)
    group = [wide[8 * g : 8 * g + 8, :] for g in range(n_groups)]
    step = 4
    for first in range(0, width, step):
        g0 = first // 8
        live = range(g0, n_groups)
        columns = [
            {
                g: jnp.broadcast_to(group[g][:, first + k : first + k + 1], (8, 2 * width))
                for g in live
            }
            for k in range(step)
        ]
        for k in range(step):
            r = (first + k) % 8
            pivot_row = group[g0][r : r + 1, :]
            pivot = columns[k][g0][r : r + 1, :]
            inverse = 1.0 / pivot
            out_ref[first + k : first + k + 1, :] = pivot_row * lax.rsqrt(pivot)
            scaled_row = pivot_row * inverse
            heads = [columns[l][g0][r : r + 1, :] * inverse for l in range(k + 1, step)]
            for g in live:
                factor = columns[k][g]
                if g == g0:
                    factor = jnp.where(sublane > r, factor, 0.0)
                group[g] = group[g] - factor * scaled_row
                for l in range(k + 1, step):
                    columns[l][g] = columns[l][g] - factor * heads[l - k - 1]


def write_upper(root_rows, wide_ref, upper_ref):
    width = upper_ref.shape[0]
    row = lax.broadcasted_iota(jnp.int32, (width, width), 0)
    column = lax.broadcasted_iota(jnp.int32, (width, width), 1)
    wide = wide_ref[...]
    upper_ref[...] = jnp.where(column >= row, wide[:, :width], 0.0) * (1.0 / root_rows)
    high, low = halves(wide[:, width:])
    return jnp.concatenate([high, high, low, low], axis=1)


def applied_inverse(stacked, values):
    high, low = halves(values)
    return jnp.dot(
        stacked,
        jnp.concatenate([high, low, high, low], axis=0),
        preferred_element_type=jnp.float32,
    )


def write_projection(root_rows, stacked, sums_ref, proj_ref, block):
    width = stacked.shape[0]
    start = block * LANES
    count = min(LANES, proj_ref.shape[1] - start)
    result = applied_inverse(stacked, sums_ref[block * width : (block + 1) * width, :])
    proj_ref[:, start : start + count] = (result * (1.0 / root_rows))[:, :count]


def write_basis(root_rows, stacked, panel_ref, basis_ref):
    for start in range(0, panel_ref.shape[1], BATCH):
        basis_ref[:, start : start + BATCH] = (
            applied_inverse(stacked, panel_ref[:, start : start + BATCH]) * root_rows
        )


def ordered_sum(own_ref, slots_ref, me, count):
    result = jnp.zeros(own_ref.shape, own_ref.dtype)
    for source in range(count):
        back = lax.rem(me - source + count, count)
        taken = slots_ref[lax.max(back - 1, 0)]
        result = result + jnp.where(back == 0, own_ref[...], taken)
    return result


def sum_kernel(
    n_gx,
    n_gy,
    root_rows,
    panel_ref,
    following_ref,
    basis_ref,
    upper_ref,
    proj_ref,
    wide_ref,
    basis_vmem,
    panel_vmem,
    rows_vmem,
    panel_split,
    part,
    gram_own,
    gram_gy,
    gram_mid,
    gram_gx,
    half_in,
    half_sum,
    piece_in,
    total,
    load_panel_sem,
    store_sem,
    load_sem,
    gy_send,
    gy_recv,
    gx_send,
    gx_recv,
    half_send,
    half_recv,
    rs_send,
    rs_recv,
    ag_send,
    ag_recv,
    back_send,
    back_recv,
):
    width = panel_ref.shape[0]
    units = rows_vmem.shape[0] // width
    half_rows = rows_vmem.shape[0] // LANES * width // 2
    group_rows = BATCH // LANES * width
    n_groups = half_rows // group_rows
    n_chips = n_gx * n_gy // 2
    piece = group_rows // n_chips
    me_x, me_y = lax.axis_index("gx"), lax.axis_index("gy")
    core = lax.rem(me_y, 2)
    other = 1 - core
    chip = me_x * (n_gy // 2) + me_y // 2
    sibling = (me_x, me_y + 1 - 2 * core)

    def chip_device(index):
        return (index // (n_gy // 2), lax.rem(index, n_gy // 2) * 2 + core)

    load_panel = pltpu.make_async_copy(panel_ref, panel_vmem, load_panel_sem)
    load_panel.start()

    def load(source, unit):
        pltpu.make_async_copy(
            source, rows_vmem.at[pl.ds(unit * width, width)], load_sem.at[unit]
        ).start()

    batch_units = BATCH // width
    for group in range(n_groups):
        for half in (other, core):
            for k in range(batch_units):
                unit = (half * n_groups + group) * batch_units + k
                if group < n_groups - 1 or k < batch_units - 1:
                    load(following_ref.at[pl.ds(unit * width, width)], unit)
                    continue

                @pl.when(half == 1)
                def _():
                    load(panel_ref, units - 1)

                @pl.when(half == 0)
                def _():
                    load(following_ref.at[pl.ds((units // 2 - 1) * width, width)], units // 2 - 1)

    barrier = pltpu.get_barrier_semaphore()
    n_signals = 0
    for k in range(1, n_chips):
        pl.semaphore_signal(
            barrier, inc=1, device_id=chip_device(lax.rem(chip + k, n_chips)), device_id_type=MESH
        )
        n_signals += 1
    for k in range(1, n_gy, 2):
        pl.semaphore_signal(
            barrier, inc=1, device_id=(me_x, lax.rem(me_y + k, n_gy)), device_id_type=MESH
        )
        n_signals += 1

    load_panel.wait()
    high, low = halves(panel_vmem[...])
    panel_split[0:width, :] = high
    panel_split[width : 2 * width, :] = low
    quads = rows_product(panel_split[...], panel_split[...])
    pair = quads[:width] + quads[width:]
    gram = pair[:, :width] + pair[:, width:]
    gram_own[...] = jnp.concatenate([gram[: width // 2], gram[width // 2 :]], axis=1)

    pl.semaphore_wait(barrier, n_signals)

    gy_copies = []
    for k in range(1, n_gy):
        copy = pltpu.make_async_remote_copy(
            src_ref=gram_own,
            dst_ref=gram_gy.at[k - 1],
            send_sem=gy_send.at[k - 1],
            recv_sem=gy_recv.at[k - 1],
            device_id=(me_x, lax.rem(me_y + k, n_gy)),
            device_id_type=MESH,
        )
        copy.start()
        gy_copies.append(copy)

    def cross(half, group):
        index = half * n_groups + group
        for k in range(batch_units):
            unit = index * batch_units + k
            pltpu.make_async_copy(
                panel_ref, rows_vmem.at[pl.ds(unit * width, width)], load_sem.at[unit]
            ).wait()
        row_high, row_low = halves(rows_vmem[pl.ds(index * BATCH, BATCH), :])
        quads = rows_product(jnp.concatenate([row_high, row_low], axis=0), panel_split[...])
        pair = quads[:BATCH] + quads[BATCH:]
        for k in range(BATCH // LANES):
            turned = pair[k * LANES : (k + 1) * LANES].T
            part[pl.ds(index * group_rows + k * width, width), :] = turned[:width] + turned[width:]

    half_copies, rs_copies, ag_copies, back_copies = [], [], [], []

    def start_half(group):
        copy = pltpu.make_async_remote_copy(
            src_ref=part.at[pl.ds(other * half_rows + group * group_rows, group_rows)],
            dst_ref=half_in.at[pl.ds(group * group_rows, group_rows)],
            send_sem=half_send.at[group],
            recv_sem=half_recv.at[group],
            device_id=sibling,
            device_id_type=MESH,
        )
        copy.start()
        half_copies.append(copy)

    def start_scatter(group):
        half_copies[group].wait_recv()
        start = group * group_rows
        half_sum[start : start + group_rows, :] = (
            part[pl.ds(core * half_rows + start, group_rows), :]
            + half_in[start : start + group_rows, :]
        )
        copies = []
        for k in range(1, n_chips):
            to = lax.rem(chip + k, n_chips)
            copy = pltpu.make_async_remote_copy(
                src_ref=half_sum.at[pl.ds(start + to * piece, piece)],
                dst_ref=piece_in.at[group, k - 1],
                send_sem=rs_send.at[group, k - 1],
                recv_sem=rs_recv.at[group, k - 1],
                device_id=chip_device(to),
                device_id_type=MESH,
            )
            copy.start()
            copies.append(copy)
        rs_copies.append(copies)

    def start_gather(group):
        for copy in rs_copies[group]:
            copy.wait_recv()
        own = half_sum[pl.ds(group * group_rows + chip * piece, piece), :]
        for k in range(n_chips - 1):
            own = own + piece_in[group, k]
        start = core * half_rows + group * group_rows + chip * piece
        total[pl.ds(start, piece), :] = own
        copies = []
        for k in range(1, n_chips):
            copy = pltpu.make_async_remote_copy(
                src_ref=total.at[pl.ds(start, piece)],
                dst_ref=total.at[pl.ds(start, piece)],
                send_sem=ag_send.at[group, k - 1],
                recv_sem=ag_recv.at[group, k - 1],
                device_id=chip_device(lax.rem(chip + k, n_chips)),
                device_id_type=MESH,
            )
            copy.start()
            copies.append(copy)
        ag_copies.append(copies)

    def start_back(group):
        for copy in ag_copies[group]:
            copy.wait_recv()
        start = core * half_rows + group * group_rows
        copy = pltpu.make_async_remote_copy(
            src_ref=total.at[pl.ds(start, group_rows)],
            dst_ref=total.at[pl.ds(start, group_rows)],
            send_sem=back_send.at[group],
            recv_sem=back_recv.at[group],
            device_id=sibling,
            device_id_type=MESH,
        )
        copy.start()
        back_copies.append(copy)

    gx_copies = []
    for group in range(n_groups):
        cross(other, group)
        start_half(group)
        if group == 0:
            for copy in gy_copies:
                copy.wait_recv()
            gram_mid[...] = ordered_sum(gram_own, gram_gy, me_y, n_gy)
            for k in range(1, n_gx):
                copy = pltpu.make_async_remote_copy(
                    src_ref=gram_mid,
                    dst_ref=gram_gx.at[k - 1],
                    send_sem=gx_send.at[k - 1],
                    recv_sem=gx_recv.at[k - 1],
                    device_id=(lax.rem(me_x + k, n_gx), me_y),
                    device_id_type=MESH,
                )
                copy.start()
                gx_copies.append(copy)
        cross(core, group)
        start_scatter(group)
    for group in range(n_groups - 1):
        start_gather(group)

    for copy in gx_copies:
        copy.wait_recv()
    packed = ordered_sum(gram_mid, gram_gx, me_x, n_gx)
    eliminate(jnp.concatenate([packed[:, :width], packed[:, width:]], axis=0), wide_ref)
    start_gather(n_groups - 1)

    stacked = write_upper(root_rows, wide_ref, upper_ref)
    write_basis(root_rows, stacked, panel_vmem, basis_vmem)
    store = pltpu.make_async_copy(basis_vmem, basis_ref, store_sem)
    store.start()
    for group in range(n_groups):
        start_back(group)
    for group in range(n_groups):
        back_copies[group].wait_recv()
        for half in range(2):
            for k in range(BATCH // LANES):
                block = (half * n_groups + group) * (BATCH // LANES) + k
                write_projection(root_rows, stacked, total, proj_ref, block)
    store.wait()
    for copies in rs_copies + ag_copies + [gy_copies, gx_copies, half_copies, back_copies]:
        for copy in copies:
            copy.wait_send()


def exchanged(panel, following, n_gx, n_gy, root_rows):
    width, cells = panel.shape
    rows = width + following.shape[0]
    all_rows = rows // LANES * width
    half_rows = all_rows // 2
    group_rows = BATCH // LANES * width
    n_groups = half_rows // group_rows
    n_chips = n_gx * n_gy // 2
    piece = group_rows // n_chips
    gram_block = (width // 2, 2 * width)
    dma = pltpu.SemaphoreType.DMA
    f32 = jnp.float32
    return pl.pallas_call(
        functools.partial(sum_kernel, n_gx, n_gy, root_rows),
        out_shape=(
            jax.ShapeDtypeStruct((width, cells), f32),
            jax.ShapeDtypeStruct((width, width), f32),
            jax.ShapeDtypeStruct((width, following.shape[0]), f32),
        ),
        in_specs=[pl.BlockSpec(memory_space=pltpu.HBM)] * 2,
        out_specs=(
            pl.BlockSpec(memory_space=pl.ANY),
            pl.BlockSpec(memory_space=pltpu.VMEM),
            pl.BlockSpec(memory_space=pltpu.VMEM),
        ),
        scratch_shapes=[
            pltpu.VMEM((width, 2 * width), f32),
            pltpu.VMEM((width, cells), f32),
            pltpu.VMEM((width, cells), f32),
            pltpu.VMEM((rows, cells), f32),
            pltpu.VMEM((2 * width, cells), jnp.bfloat16),
            pltpu.VMEM((all_rows, LANES), f32),
            pltpu.VMEM(gram_block, f32),
            pltpu.VMEM((n_gy - 1,) + gram_block, f32),
            pltpu.VMEM(gram_block, f32),
            pltpu.VMEM((n_gx - 1,) + gram_block, f32),
            pltpu.VMEM((half_rows, LANES), f32),
            pltpu.VMEM((half_rows, LANES), f32),
            pltpu.VMEM((n_groups, n_chips - 1, piece, LANES), f32),
            pltpu.VMEM((all_rows, LANES), f32),
            dma,
            dma,
            dma((rows // width,)),
            dma((n_gy - 1,)),
            dma((n_gy - 1,)),
            dma((n_gx - 1,)),
            dma((n_gx - 1,)),
            dma((n_groups,)),
            dma((n_groups,)),
            dma((n_groups, n_chips - 1)),
            dma((n_groups, n_chips - 1)),
            dma((n_groups, n_chips - 1)),
            dma((n_groups, n_chips - 1)),
            dma((n_groups,)),
            dma((n_groups,)),
        ],
        compiler_params=pltpu.CompilerParams(
            collective_id=0, has_side_effects=True, vmem_limit_bytes=56 * 2**20
        ),
        name="sum_and_factor",
    )(panel, following)


def apply_kernel(root_rows, sums_ref, wide_ref, panel_ref, basis_ref, upper_ref, proj_ref):
    stacked = write_upper(root_rows, wide_ref, upper_ref)
    for block in range(sums_ref.shape[0] // panel_ref.shape[0]):
        write_projection(root_rows, stacked, sums_ref, proj_ref, block)
    write_basis(root_rows, stacked, panel_ref, basis_ref)


def applied(sums, wide, panel, next_count, root_rows):
    width, cells = panel.shape
    f32 = jnp.float32
    return pl.pallas_call(
        functools.partial(apply_kernel, root_rows),
        out_shape=(
            jax.ShapeDtypeStruct((width, cells), f32),
            jax.ShapeDtypeStruct((width, width), f32),
            jax.ShapeDtypeStruct((width, next_count), f32),
        ),
        compiler_params=pltpu.CompilerParams(vmem_limit_bytes=60 * 2**20),
        name="apply_factor",
    )(sums, wide, panel)


def plain_sums(panel, following):
    precise = functools.partial(
        lax.dot_general,
        dimension_numbers=(((1,), (1,)), ((), ())),
        precision=lax.Precision.HIGHEST,
        preferred_element_type=jnp.float32,
    )
    width = panel.shape[0]
    cross = lax.psum(
        jnp.concatenate([precise(panel, following), precise(panel, panel)], axis=1), ("gx", "gy")
    )
    blocks = cross.shape[1] // LANES
    sums = cross.reshape(width, blocks, LANES).transpose(1, 0, 2).reshape(blocks * width, LANES)
    wide = pl.pallas_call(
        lambda gram_ref, wide_ref: eliminate(gram_ref[...], wide_ref),
        out_shape=jax.ShapeDtypeStruct((width, 2 * width), jnp.float32),
        name="factor",
    )(cross[:, -width:])
    return sums, wide


def body(n_gx, n_gy, panel, following):
    width, cells = panel.shape
    root_rows = math.sqrt(cells * n_gx * n_gy)
    if BATCH // LANES * width % (8 * (n_gx * n_gy // 2)) == 0:
        return exchanged(panel, following, n_gx, n_gy, root_rows)
    sums, wide = plain_sums(panel, following)
    return applied(sums, wide, panel, following.shape[0], root_rows)


def solution(mesh):
    return jax.shard_map(
        functools.partial(body, mesh.shape["gx"], mesh.shape["gy"]),
        mesh=mesh,
        in_specs=(P(None, ("gx", "gy")), P(None, ("gx", "gy"))),
        out_specs=(P(None, ("gx", "gy")), P(), P()),
        check_vma=False,
    )
```

```python
import functools
import math

import jax
import jax.numpy as jnp
from jax import lax
from jax.experimental import pallas as pl
from jax.experimental.pallas import tpu as pltpu
from jax.sharding import PartitionSpec as P

MESH = pl.DeviceIdType.MESH
LANES = 128
BATCH = 256
CELLS = 512


def halves(values):
    high = values.astype(jnp.bfloat16)
    return high, (values - high.astype(jnp.float32)).astype(jnp.bfloat16)


def product(left, right):
    return jnp.dot(left, right, preferred_element_type=jnp.float32)


def eliminate(gram, out_ref):
    width = gram.shape[0]
    row = lax.broadcasted_iota(jnp.int32, (width, width), 0)
    column = lax.broadcasted_iota(jnp.int32, (width, width), 1)
    wide = jnp.concatenate([gram, jnp.where(row == column, 1.0, 0.0)], axis=1)
    n_groups = width // 8
    sublane = lax.broadcasted_iota(jnp.int32, (8, 2 * width), 0)
    group = [wide[8 * g : 8 * g + 8, :] for g in range(n_groups)]
    step = 4
    for first in range(0, width, step):
        g0 = first // 8
        live = range(g0, n_groups)
        columns = [
            {
                g: jnp.broadcast_to(group[g][:, first + k : first + k + 1], (8, 2 * width))
                for g in live
            }
            for k in range(step)
        ]
        for k in range(step):
            r = (first + k) % 8
            pivot_row = group[g0][r : r + 1, :]
            pivot = columns[k][g0][r : r + 1, :]
            inverse = 1.0 / pivot
            out_ref[first + k : first + k + 1, :] = pivot_row * lax.rsqrt(pivot)
            scaled_row = pivot_row * inverse
            heads = [columns[l][g0][r : r + 1, :] * inverse for l in range(k + 1, step)]
            for g in live:
                factor = columns[k][g]
                if g == g0:
                    factor = jnp.where(sublane > r, factor, 0.0)
                group[g] = group[g] - factor * scaled_row
                for l in range(k + 1, step):
                    columns[l][g] = columns[l][g] - factor * heads[l - k - 1]


def write_upper(root_rows, wide_ref, upper_ref):
    width = upper_ref.shape[0]
    row = lax.broadcasted_iota(jnp.int32, (width, width), 0)
    column = lax.broadcasted_iota(jnp.int32, (width, width), 1)
    wide = wide_ref[...]
    upper_ref[...] = jnp.where(column >= row, wide[:, :width], 0.0) * (1.0 / root_rows)
    high, low = halves(wide[:, width:])
    return jnp.concatenate([high, high, low, low], axis=1)


def applied_inverse(stacked, values):
    high, low = halves(values)
    return jnp.dot(
        stacked,
        jnp.concatenate([high, low, high, low], axis=0),
        preferred_element_type=jnp.float32,
    )


def write_projection(root_rows, stacked, sums_ref, proj_ref, block):
    width = stacked.shape[0]
    start = block * LANES
    count = min(LANES, proj_ref.shape[1] - start)
    result = applied_inverse(stacked, sums_ref[block * width : (block + 1) * width, :])
    proj_ref[:, start : start + count] = (result * (1.0 / root_rows))[:, :count]


def write_basis(root_rows, stacked, panel_ref, basis_ref):
    for start in range(0, panel_ref.shape[1], BATCH):
        basis_ref[:, start : start + BATCH] = (
            applied_inverse(stacked, panel_ref[:, start : start + BATCH]) * root_rows
        )


def ordered_sum(own_ref, slots_ref, me, count):
    result = jnp.zeros(own_ref.shape, own_ref.dtype)
    for source in range(count):
        back = lax.rem(me - source + count, count)
        taken = slots_ref[lax.max(back - 1, 0)]
        result = result + jnp.where(back == 0, own_ref[...], taken)
    return result


def sum_kernel(
    n_gx,
    n_gy,
    panel_ref,
    following_ref,
    sums_ref,
    wide_ref,
    panel_vmem,
    rows_vmem,
    panel_turned,
    part,
    gram_own,
    gram_gy,
    gram_mid,
    gram_gx,
    half_in,
    half_sum,
    piece_in,
    total,
    load_panel_sem,
    load_sem,
    gy_send,
    gy_recv,
    gx_send,
    gx_recv,
    half_send,
    half_recv,
    rs_send,
    rs_recv,
    ag_send,
    ag_recv,
    back_send,
    back_recv,
):
    width = panel_ref.shape[0]
    units = rows_vmem.shape[0] // width
    half_rows = rows_vmem.shape[0] // LANES * width // 2
    group_rows = BATCH // LANES * width
    n_groups = half_rows // group_rows
    n_chips = n_gx * n_gy // 2
    piece = group_rows // n_chips
    me_x, me_y = lax.axis_index("gx"), lax.axis_index("gy")
    core = lax.rem(me_y, 2)
    other = 1 - core
    chip = me_x * (n_gy // 2) + me_y // 2
    sibling = (me_x, me_y + 1 - 2 * core)

    def chip_device(index):
        return (index // (n_gy // 2), lax.rem(index, n_gy // 2) * 2 + core)

    load_panel = pltpu.make_async_copy(panel_ref, panel_vmem, load_panel_sem)
    load_panel.start()

    def load(source, unit):
        pltpu.make_async_copy(
            source, rows_vmem.at[pl.ds(unit * width, width)], load_sem.at[unit]
        ).start()

    batch_units = BATCH // width
    for group in range(n_groups):
        for half in (other, core):
            for k in range(batch_units):
                unit = (half * n_groups + group) * batch_units + k
                if group < n_groups - 1 or k < batch_units - 1:
                    load(following_ref.at[pl.ds(unit * width, width)], unit)
                    continue

                @pl.when(half == 1)
                def _():
                    load(panel_ref, units - 1)

                @pl.when(half == 0)
                def _():
                    load(following_ref.at[pl.ds((units // 2 - 1) * width, width)], units // 2 - 1)

    barrier = pltpu.get_barrier_semaphore()
    n_signals = 0
    for k in range(1, n_chips):
        pl.semaphore_signal(
            barrier, inc=1, device_id=chip_device(lax.rem(chip + k, n_chips)), device_id_type=MESH
        )
        n_signals += 1
    for k in range(1, n_gy, 2):
        pl.semaphore_signal(
            barrier, inc=1, device_id=(me_x, lax.rem(me_y + k, n_gy)), device_id_type=MESH
        )
        n_signals += 1

    load_panel.wait()
    panel = panel_vmem[...]
    high = panel.astype(jnp.bfloat16).astype(jnp.float32)
    split = jnp.concatenate([high, panel - high], axis=0)
    panel_turned[...] = split.T.astype(jnp.bfloat16)
    quads = product(split.astype(jnp.bfloat16), panel_turned[...])
    pair = quads[:width] + quads[width:]
    gram = pair[:, :width] + pair[:, width:]
    gram_own[...] = jnp.concatenate([gram[: width // 2], gram[width // 2 :]], axis=1)

    pl.semaphore_wait(barrier, n_signals)

    gy_copies = []
    for k in range(1, n_gy):
        copy = pltpu.make_async_remote_copy(
            src_ref=gram_own,
            dst_ref=gram_gy.at[k - 1],
            send_sem=gy_send.at[k - 1],
            recv_sem=gy_recv.at[k - 1],
            device_id=(me_x, lax.rem(me_y + k, n_gy)),
            device_id_type=MESH,
        )
        copy.start()
        gy_copies.append(copy)

    def cross(half, group):
        index = half * n_groups + group
        for k in range(batch_units):
            unit = index * batch_units + k
            pltpu.make_async_copy(
                panel_ref, rows_vmem.at[pl.ds(unit * width, width)], load_sem.at[unit]
            ).wait()
        pair = jnp.zeros((BATCH, 2 * width), jnp.float32)
        for start in range(0, rows_vmem.shape[1], CELLS):
            rows = rows_vmem[pl.ds(index * BATCH, BATCH), start : start + CELLS]
            quads = product(
                jnp.concatenate(halves(rows), axis=0), panel_turned[start : start + CELLS, :]
            )
            pair = pair + (quads[:BATCH] + quads[BATCH:])
        for k in range(BATCH // LANES):
            turned = pair[k * LANES : (k + 1) * LANES].T
            part[pl.ds(index * group_rows + k * width, width), :] = turned[:width] + turned[width:]

    half_copies, rs_copies, ag_copies, back_copies = [], [], [], []

    def start_half(group):
        copy = pltpu.make_async_remote_copy(
            src_ref=part.at[pl.ds(other * half_rows + group * group_rows, group_rows)],
            dst_ref=half_in.at[pl.ds(group * group_rows, group_rows)],
            send_sem=half_send.at[group],
            recv_sem=half_recv.at[group],
            device_id=sibling,
            device_id_type=MESH,
        )
        copy.start()
        half_copies.append(copy)

    def start_scatter(group):
        half_copies[group].wait_recv()
        start = group * group_rows
        half_sum[start : start + group_rows, :] = (
            part[pl.ds(core * half_rows + start, group_rows), :]
            + half_in[start : start + group_rows, :]
        )
        copies = []
        for k in range(1, n_chips):
            to = lax.rem(chip + k, n_chips)
            copy = pltpu.make_async_remote_copy(
                src_ref=half_sum.at[pl.ds(start + to * piece, piece)],
                dst_ref=piece_in.at[group, k - 1],
                send_sem=rs_send.at[group, k - 1],
                recv_sem=rs_recv.at[group, k - 1],
                device_id=chip_device(to),
                device_id_type=MESH,
            )
            copy.start()
            copies.append(copy)
        rs_copies.append(copies)

    def start_gather(group):
        for copy in rs_copies[group]:
            copy.wait_recv()
        own = half_sum[pl.ds(group * group_rows + chip * piece, piece), :]
        for k in range(n_chips - 1):
            own = own + piece_in[group, k]
        start = core * half_rows + group * group_rows + chip * piece
        total[pl.ds(start, piece), :] = own
        copies = []
        for k in range(1, n_chips):
            copy = pltpu.make_async_remote_copy(
                src_ref=total.at[pl.ds(start, piece)],
                dst_ref=total.at[pl.ds(start, piece)],
                send_sem=ag_send.at[group, k - 1],
                recv_sem=ag_recv.at[group, k - 1],
                device_id=chip_device(lax.rem(chip + k, n_chips)),
                device_id_type=MESH,
            )
            copy.start()
            copies.append(copy)
        ag_copies.append(copies)

    def start_back(group):
        for copy in ag_copies[group]:
            copy.wait_recv()
        start = core * half_rows + group * group_rows
        copy = pltpu.make_async_remote_copy(
            src_ref=total.at[pl.ds(start, group_rows)],
            dst_ref=total.at[pl.ds(start, group_rows)],
            send_sem=back_send.at[group],
            recv_sem=back_recv.at[group],
            device_id=sibling,
            device_id_type=MESH,
        )
        copy.start()
        back_copies.append(copy)

    gx_copies = []
    for group in range(n_groups):
        cross(other, group)
        start_half(group)
        if group == 0:
            for copy in gy_copies:
                copy.wait_recv()
            gram_mid[...] = ordered_sum(gram_own, gram_gy, me_y, n_gy)
            for k in range(1, n_gx):
                copy = pltpu.make_async_remote_copy(
                    src_ref=gram_mid,
                    dst_ref=gram_gx.at[k - 1],
                    send_sem=gx_send.at[k - 1],
                    recv_sem=gx_recv.at[k - 1],
                    device_id=(lax.rem(me_x + k, n_gx), me_y),
                    device_id_type=MESH,
                )
                copy.start()
                gx_copies.append(copy)
        cross(core, group)
        start_scatter(group)
    for group in range(n_groups - 1):
        start_gather(group)

    for copy in gx_copies:
        copy.wait_recv()
    packed = ordered_sum(gram_mid, gram_gx, me_x, n_gx)
    eliminate(jnp.concatenate([packed[:, :width], packed[:, width:]], axis=0), wide_ref)
    start_gather(n_groups - 1)

    for group in range(n_groups):
        start_back(group)
    for copy in back_copies:
        copy.wait_recv()
    sums_ref[...] = total[...]
    for copies in rs_copies + ag_copies + [gy_copies, gx_copies, half_copies, back_copies]:
        for copy in copies:
            copy.wait_send()


def exchanged(panel, following, n_gx, n_gy):
    width, cells = panel.shape
    rows = width + following.shape[0]
    all_rows = rows // LANES * width
    half_rows = all_rows // 2
    group_rows = BATCH // LANES * width
    n_groups = half_rows // group_rows
    n_chips = n_gx * n_gy // 2
    piece = group_rows // n_chips
    gram_block = (width // 2, 2 * width)
    dma = pltpu.SemaphoreType.DMA
    f32 = jnp.float32
    return pl.pallas_call(
        functools.partial(sum_kernel, n_gx, n_gy),
        out_shape=(
            jax.ShapeDtypeStruct((all_rows, LANES), f32),
            jax.ShapeDtypeStruct((width, 2 * width), f32),
        ),
        in_specs=[pl.BlockSpec(memory_space=pltpu.HBM)] * 2,
        out_specs=(
            pl.BlockSpec(memory_space=pltpu.VMEM),
            pl.BlockSpec(memory_space=pltpu.VMEM),
        ),
        scratch_shapes=[
            pltpu.VMEM((width, cells), f32),
            pltpu.VMEM((rows, cells), f32),
            pltpu.VMEM((cells, 2 * width), jnp.bfloat16),
            pltpu.VMEM((all_rows, LANES), f32),
            pltpu.VMEM(gram_block, f32),
            pltpu.VMEM((n_gy - 1,) + gram_block, f32),
            pltpu.VMEM(gram_block, f32),
            pltpu.VMEM((n_gx - 1,) + gram_block, f32),
            pltpu.VMEM((half_rows, LANES), f32),
            pltpu.VMEM((half_rows, LANES), f32),
            pltpu.VMEM((n_groups, n_chips - 1, piece, LANES), f32),
            pltpu.VMEM((all_rows, LANES), f32),
            dma,
            dma((rows // width,)),
            dma((n_gy - 1,)),
            dma((n_gy - 1,)),
            dma((n_gx - 1,)),
            dma((n_gx - 1,)),
            dma((n_groups,)),
            dma((n_groups,)),
            dma((n_groups, n_chips - 1)),
            dma((n_groups, n_chips - 1)),
            dma((n_groups, n_chips - 1)),
            dma((n_groups, n_chips - 1)),
            dma((n_groups,)),
            dma((n_groups,)),
        ],
        compiler_params=pltpu.CompilerParams(
            collective_id=0, has_side_effects=True, vmem_limit_bytes=56 * 2**20
        ),
        name="sum_and_factor",
    )(panel, following)


def apply_kernel(root_rows, sums_ref, wide_ref, panel_ref, basis_ref, upper_ref, proj_ref):
    stacked = write_upper(root_rows, wide_ref, upper_ref)
    for block in range(sums_ref.shape[0] // panel_ref.shape[0]):
        write_projection(root_rows, stacked, sums_ref, proj_ref, block)
    write_basis(root_rows, stacked, panel_ref, basis_ref)


def applied(sums, wide, panel, next_count, root_rows):
    width, cells = panel.shape
    f32 = jnp.float32
    return pl.pallas_call(
        functools.partial(apply_kernel, root_rows),
        out_shape=(
            jax.ShapeDtypeStruct((width, cells), f32),
            jax.ShapeDtypeStruct((width, width), f32),
            jax.ShapeDtypeStruct((width, next_count), f32),
        ),
        compiler_params=pltpu.CompilerParams(vmem_limit_bytes=60 * 2**20),
        name="apply_factor",
    )(sums, wide, panel)


def plain_sums(panel, following):
    precise = functools.partial(
        lax.dot_general,
        dimension_numbers=(((1,), (1,)), ((), ())),
        precision=lax.Precision.HIGHEST,
        preferred_element_type=jnp.float32,
    )
    width = panel.shape[0]
    cross = lax.psum(
        jnp.concatenate([precise(panel, following), precise(panel, panel)], axis=1), ("gx", "gy")
    )
    blocks = cross.shape[1] // LANES
    sums = cross.reshape(width, blocks, LANES).transpose(1, 0, 2).reshape(blocks * width, LANES)
    wide = pl.pallas_call(
        lambda gram_ref, wide_ref: eliminate(gram_ref[...], wide_ref),
        out_shape=jax.ShapeDtypeStruct((width, 2 * width), jnp.float32),
        name="factor",
    )(cross[:, -width:])
    return sums, wide


def body(n_gx, n_gy, panel, following):
    width, cells = panel.shape
    root_rows = math.sqrt(cells * n_gx * n_gy)
    if BATCH // LANES * width % (8 * (n_gx * n_gy // 2)) == 0:
        sums, wide = exchanged(panel, following, n_gx, n_gy)
    else:
        sums, wide = plain_sums(panel, following)
    return applied(sums, wide, panel, following.shape[0], root_rows)


def solution(mesh):
    return jax.shard_map(
        functools.partial(body, mesh.shape["gx"], mesh.shape["gy"]),
        mesh=mesh,
        in_specs=(P(None, ("gx", "gy")), P(None, ("gx", "gy"))),
        out_specs=(P(None, ("gx", "gy")), P(), P()),
        check_vma=False,
    )
```

```python
import functools
import math

import jax
import jax.numpy as jnp
from jax import lax
from jax.experimental import pallas as pl
from jax.experimental.pallas import tpu as pltpu
from jax.sharding import PartitionSpec as P

MESH = pl.DeviceIdType.MESH
LANES = 128
BATCH = 256
CELLS = 512


def halves(values):
    high = values.astype(jnp.bfloat16)
    return high, (values - high.astype(jnp.float32)).astype(jnp.bfloat16)


def product(left, right):
    return jnp.dot(left, right, preferred_element_type=jnp.float32)


def eliminate(gram, out_ref):
    width = gram.shape[0]
    row = lax.broadcasted_iota(jnp.int32, (width, width), 0)
    column = lax.broadcasted_iota(jnp.int32, (width, width), 1)
    wide = jnp.concatenate([gram, jnp.where(row == column, 1.0, 0.0)], axis=1)
    n_groups = width // 8
    sublane = lax.broadcasted_iota(jnp.int32, (8, 2 * width), 0)
    group = [wide[8 * g : 8 * g + 8, :] for g in range(n_groups)]
    step = 4
    for first in range(0, width, step):
        g0 = first // 8
        live = range(g0, n_groups)
        columns = [
            {
                g: jnp.broadcast_to(group[g][:, first + k : first + k + 1], (8, 2 * width))
                for g in live
            }
            for k in range(step)
        ]
        for k in range(step):
            r = (first + k) % 8
            pivot_row = group[g0][r : r + 1, :]
            pivot = columns[k][g0][r : r + 1, :]
            inverse = 1.0 / pivot
            out_ref[first + k : first + k + 1, :] = pivot_row * lax.rsqrt(pivot)
            scaled_row = pivot_row * inverse
            heads = [columns[l][g0][r : r + 1, :] * inverse for l in range(k + 1, step)]
            for g in live:
                factor = columns[k][g]
                if g == g0:
                    factor = jnp.where(sublane > r, factor, 0.0)
                group[g] = group[g] - factor * scaled_row
                for l in range(k + 1, step):
                    columns[l][g] = columns[l][g] - factor * heads[l - k - 1]


def write_upper(root_rows, wide_ref, upper_ref):
    width = upper_ref.shape[0]
    row = lax.broadcasted_iota(jnp.int32, (width, width), 0)
    column = lax.broadcasted_iota(jnp.int32, (width, width), 1)
    wide = wide_ref[...]
    upper_ref[...] = jnp.where(column >= row, wide[:, :width], 0.0) * (1.0 / root_rows)
    high, low = halves(wide[:, width:])
    return jnp.concatenate([high, high, low, low], axis=1)


def applied_inverse(stacked, values):
    high, low = halves(values)
    return jnp.dot(
        stacked,
        jnp.concatenate([high, low, high, low], axis=0),
        preferred_element_type=jnp.float32,
    )


def write_projection(root_rows, stacked, sums_ref, proj_ref, block):
    width = stacked.shape[0]
    start = block * LANES
    count = min(LANES, proj_ref.shape[1] - start)
    result = applied_inverse(stacked, sums_ref[block * width : (block + 1) * width, :])
    proj_ref[:, start : start + count] = (result * (1.0 / root_rows))[:, :count]


def write_basis(root_rows, stacked, panel_ref, basis_ref):
    for start in range(0, panel_ref.shape[1], BATCH):
        basis_ref[:, start : start + BATCH] = (
            applied_inverse(stacked, panel_ref[:, start : start + BATCH]) * root_rows
        )


def ordered_sum(own_ref, slots_ref, me, count):
    result = jnp.zeros(own_ref.shape, own_ref.dtype)
    for source in range(count):
        back = lax.rem(me - source + count, count)
        taken = slots_ref[lax.max(back - 1, 0)]
        result = result + jnp.where(back == 0, own_ref[...], taken)
    return result


def sum_kernel(
    n_gx,
    n_gy,
    panel_ref,
    following_ref,
    sums_ref,
    wide_ref,
    panel_vmem,
    rows_vmem,
    panel_turned,
    part,
    gram_own,
    gram_gy,
    gram_mid,
    gram_gx,
    half_in,
    half_sum,
    piece_in,
    total,
    load_panel_sem,
    load_sem,
    gy_send,
    gy_recv,
    gx_send,
    gx_recv,
    half_send,
    half_recv,
    rs_send,
    rs_recv,
    ag_send,
    ag_recv,
    back_send,
    back_recv,
):
    width = panel_ref.shape[0]
    units = rows_vmem.shape[0] // width
    half_batches = rows_vmem.shape[0] // BATCH // 2
    batch_rows = BATCH // LANES * width
    half_rows = half_batches * batch_rows
    n_chips = n_gx * n_gy // 2
    piece = half_rows // n_chips
    me_x, me_y = lax.axis_index("gx"), lax.axis_index("gy")
    core = lax.rem(me_y, 2)
    other = 1 - core
    chip = me_x * (n_gy // 2) + me_y // 2
    sibling = (me_x, me_y + 1 - 2 * core)

    def chip_device(index):
        return (index // (n_gy // 2), lax.rem(index, n_gy // 2) * 2 + core)

    load_panel = pltpu.make_async_copy(panel_ref, panel_vmem, load_panel_sem)
    load_panel.start()

    @pl.loop(0, units)
    def _(step):
        unit = lax.rem(step + other * (units // 2), units)

        def load(source):
            pltpu.make_async_copy(
                source, rows_vmem.at[pl.ds(unit * width, width)], load_sem.at[unit]
            ).start()

        @pl.when(unit == units - 1)
        def _():
            load(panel_ref)

        @pl.when(unit != units - 1)
        def _():
            load(following_ref.at[pl.ds(unit * width, width)])

    barrier = pltpu.get_barrier_semaphore()

    @pl.loop(1, n_chips)
    def _(k):
        pl.semaphore_signal(
            barrier, inc=1, device_id=chip_device(lax.rem(chip + k, n_chips)), device_id_type=MESH
        )

    for k in range(1, n_gy, 2):
        pl.semaphore_signal(
            barrier, inc=1, device_id=(me_x, lax.rem(me_y + k, n_gy)), device_id_type=MESH
        )
    n_signals = n_chips - 1 + n_gy // 2

    load_panel.wait()
    panel = panel_vmem[...]
    high = panel.astype(jnp.bfloat16).astype(jnp.float32)
    split = jnp.concatenate([high, panel - high], axis=0)
    panel_turned[...] = split.T.astype(jnp.bfloat16)
    quads = product(split.astype(jnp.bfloat16), panel_turned[...])
    pair = quads[:width] + quads[width:]
    gram = pair[:, :width] + pair[:, width:]
    gram_own[...] = jnp.concatenate([gram[: width // 2], gram[width // 2 :]], axis=1)

    pl.semaphore_wait(barrier, n_signals)

    def gy_copy(k):
        return pltpu.make_async_remote_copy(
            src_ref=gram_own,
            dst_ref=gram_gy.at[k - 1],
            send_sem=gy_send.at[k - 1],
            recv_sem=gy_recv.at[k - 1],
            device_id=(me_x, lax.rem(me_y + k, n_gy)),
            device_id_type=MESH,
        )

    def gx_copy(k):
        return pltpu.make_async_remote_copy(
            src_ref=gram_mid,
            dst_ref=gram_gx.at[k - 1],
            send_sem=gx_send.at[k - 1],
            recv_sem=gx_recv.at[k - 1],
            device_id=(lax.rem(me_x + k, n_gx), me_y),
            device_id_type=MESH,
        )

    def half_copy():
        return pltpu.make_async_remote_copy(
            src_ref=part.at[pl.ds(other * half_rows, half_rows)],
            dst_ref=half_in,
            send_sem=half_send,
            recv_sem=half_recv,
            device_id=sibling,
            device_id_type=MESH,
        )

    def scatter_copy(k):
        to = lax.rem(chip + k, n_chips)
        return pltpu.make_async_remote_copy(
            src_ref=half_sum.at[pl.ds(to * piece, piece)],
            dst_ref=piece_in.at[k - 1],
            send_sem=rs_send.at[k - 1],
            recv_sem=rs_recv.at[k - 1],
            device_id=chip_device(to),
            device_id_type=MESH,
        )

    own_start = core * half_rows + chip * piece

    def gather_copy(k):
        return pltpu.make_async_remote_copy(
            src_ref=total.at[pl.ds(own_start, piece)],
            dst_ref=total.at[pl.ds(own_start, piece)],
            send_sem=ag_send.at[k - 1],
            recv_sem=ag_recv.at[k - 1],
            device_id=chip_device(lax.rem(chip + k, n_chips)),
            device_id_type=MESH,
        )

    def back_copy():
        return pltpu.make_async_remote_copy(
            src_ref=total.at[pl.ds(core * half_rows, half_rows)],
            dst_ref=total.at[pl.ds(core * half_rows, half_rows)],
            send_sem=back_send,
            recv_sem=back_recv,
            device_id=sibling,
            device_id_type=MESH,
        )

    def start_all(copy, count):
        pl.loop(1, count)(lambda k: copy(k).start())

    def receive_all(copy, count):
        pl.loop(1, count)(lambda k: copy(k).wait_recv())

    def sent_all(copy, count):
        pl.loop(1, count)(lambda k: copy(k).wait_send())

    start_all(gy_copy, n_gy)

    @pl.loop(0, 2 * half_batches)
    def _(step):
        half = lax.rem(other + step // half_batches, 2)
        index = half * half_batches + lax.rem(step, half_batches)
        for k in range(BATCH // width):
            unit = index * (BATCH // width) + k
            pltpu.make_async_copy(
                panel_ref, rows_vmem.at[pl.ds(unit * width, width)], load_sem.at[unit]
            ).wait()
        pair = jnp.zeros((BATCH, 2 * width), jnp.float32)
        for start in range(0, rows_vmem.shape[1], CELLS):
            rows = rows_vmem[pl.ds(index * BATCH, BATCH), start : start + CELLS]
            quads = product(
                jnp.concatenate(halves(rows), axis=0), panel_turned[start : start + CELLS, :]
            )
            pair = pair + (quads[:BATCH] + quads[BATCH:])
        for k in range(BATCH // LANES):
            turned = pair[k * LANES : (k + 1) * LANES].T
            part[pl.ds(index * batch_rows + k * width, width), :] = turned[:width] + turned[width:]

        @pl.when(step == half_batches - 1)
        def _():
            half_copy().start()
            receive_all(gy_copy, n_gy)
            gram_mid[...] = ordered_sum(gram_own, gram_gy, me_y, n_gy)
            start_all(gx_copy, n_gx)

    half_copy().wait_recv()
    half_sum[...] = part[pl.ds(core * half_rows, half_rows), :] + half_in[...]
    start_all(scatter_copy, n_chips)

    receive_all(gx_copy, n_gx)
    packed = ordered_sum(gram_mid, gram_gx, me_x, n_gx)
    eliminate(jnp.concatenate([packed[:, :width], packed[:, width:]], axis=0), wide_ref)

    receive_all(scatter_copy, n_chips)
    own = half_sum[pl.ds(chip * piece, piece), :]
    for k in range(n_chips - 1):
        own = own + piece_in[k]
    total[pl.ds(own_start, piece), :] = own
    start_all(gather_copy, n_chips)
    sent_all(gy_copy, n_gy)
    sent_all(gx_copy, n_gx)
    half_copy().wait_send()
    sent_all(scatter_copy, n_chips)
    receive_all(gather_copy, n_chips)
    back_copy().start()
    sent_all(gather_copy, n_chips)
    back_copy().wait_recv()
    sums_ref[...] = total[...]
    back_copy().wait_send()


def exchanged(panel, following, n_gx, n_gy):
    width, cells = panel.shape
    rows = width + following.shape[0]
    all_rows = rows // LANES * width
    half_rows = all_rows // 2
    n_chips = n_gx * n_gy // 2
    piece = half_rows // n_chips
    gram_block = (width // 2, 2 * width)
    dma = pltpu.SemaphoreType.DMA
    f32 = jnp.float32
    return pl.pallas_call(
        functools.partial(sum_kernel, n_gx, n_gy),
        out_shape=(
            jax.ShapeDtypeStruct((all_rows, LANES), f32),
            jax.ShapeDtypeStruct((width, 2 * width), f32),
        ),
        in_specs=[pl.BlockSpec(memory_space=pltpu.HBM)] * 2,
        out_specs=(
            pl.BlockSpec(memory_space=pltpu.VMEM),
            pl.BlockSpec(memory_space=pltpu.VMEM),
        ),
        scratch_shapes=[
            pltpu.VMEM((width, cells), f32),
            pltpu.VMEM((rows, cells), f32),
            pltpu.VMEM((cells, 2 * width), jnp.bfloat16),
            pltpu.VMEM((all_rows, LANES), f32),
            pltpu.VMEM(gram_block, f32),
            pltpu.VMEM((n_gy - 1,) + gram_block, f32),
            pltpu.VMEM(gram_block, f32),
            pltpu.VMEM((n_gx - 1,) + gram_block, f32),
            pltpu.VMEM((half_rows, LANES), f32),
            pltpu.VMEM((half_rows, LANES), f32),
            pltpu.VMEM((n_chips - 1, piece, LANES), f32),
            pltpu.VMEM((all_rows, LANES), f32),
            dma,
            dma((rows // width,)),
            dma((n_gy - 1,)),
            dma((n_gy - 1,)),
            dma((n_gx - 1,)),
            dma((n_gx - 1,)),
            dma,
            dma,
            dma((n_chips - 1,)),
            dma((n_chips - 1,)),
            dma((n_chips - 1,)),
            dma((n_chips - 1,)),
            dma,
            dma,
        ],
        compiler_params=pltpu.CompilerParams(
            collective_id=0, has_side_effects=True, vmem_limit_bytes=56 * 2**20
        ),
        name="sum_and_factor",
    )(panel, following)


def apply_kernel(root_rows, sums_ref, wide_ref, panel_ref, basis_ref, upper_ref, proj_ref):
    stacked = write_upper(root_rows, wide_ref, upper_ref)
    for block in range(sums_ref.shape[0] // panel_ref.shape[0]):
        write_projection(root_rows, stacked, sums_ref, proj_ref, block)
    write_basis(root_rows, stacked, panel_ref, basis_ref)


def applied(sums, wide, panel, next_count, root_rows):
    width, cells = panel.shape
    f32 = jnp.float32
    return pl.pallas_call(
        functools.partial(apply_kernel, root_rows),
        out_shape=(
            jax.ShapeDtypeStruct((width, cells), f32),
            jax.ShapeDtypeStruct((width, width), f32),
            jax.ShapeDtypeStruct((width, next_count), f32),
        ),
        compiler_params=pltpu.CompilerParams(vmem_limit_bytes=60 * 2**20),
        name="apply_factor",
    )(sums, wide, panel)


def plain_sums(panel, following):
    precise = functools.partial(
        lax.dot_general,
        dimension_numbers=(((1,), (1,)), ((), ())),
        precision=lax.Precision.HIGHEST,
        preferred_element_type=jnp.float32,
    )
    width = panel.shape[0]
    cross = lax.psum(
        jnp.concatenate([precise(panel, following), precise(panel, panel)], axis=1), ("gx", "gy")
    )
    blocks = cross.shape[1] // LANES
    sums = cross.reshape(width, blocks, LANES).transpose(1, 0, 2).reshape(blocks * width, LANES)
    wide = pl.pallas_call(
        lambda gram_ref, wide_ref: eliminate(gram_ref[...], wide_ref),
        out_shape=jax.ShapeDtypeStruct((width, 2 * width), jnp.float32),
        name="factor",
    )(cross[:, -width:])
    return sums, wide


def body(n_gx, n_gy, panel, following):
    width, cells = panel.shape
    root_rows = math.sqrt(cells * n_gx * n_gy)
    half_rows = (width + following.shape[0]) // LANES * width // 2
    if half_rows % (8 * (n_gx * n_gy // 2)) == 0:
        sums, wide = exchanged(panel, following, n_gx, n_gy)
    else:
        sums, wide = plain_sums(panel, following)
    return applied(sums, wide, panel, following.shape[0], root_rows)


def solution(mesh):
    return jax.shard_map(
        functools.partial(body, mesh.shape["gx"], mesh.shape["gy"]),
        mesh=mesh,
        in_specs=(P(None, ("gx", "gy")), P(None, ("gx", "gy"))),
        out_specs=(P(None, ("gx", "gy")), P(), P()),
        check_vma=False,
    )
```

```python
import functools
import math

import jax
import jax.numpy as jnp
from jax import lax
from jax.experimental import pallas as pl
from jax.experimental.pallas import tpu as pltpu
from jax.sharding import PartitionSpec as P

MESH = pl.DeviceIdType.MESH
LANES = 128
BATCH = 256
CELLS = 512


def halves(values):
    high = values.astype(jnp.bfloat16)
    return high, (values - high.astype(jnp.float32)).astype(jnp.bfloat16)


def product(left, right):
    return jnp.dot(left, right, preferred_element_type=jnp.float32)


def eliminate(gram, out_ref, mid_ref, begin, end):
    width = gram.shape[0]
    row = lax.broadcasted_iota(jnp.int32, (width, width), 0)
    column = lax.broadcasted_iota(jnp.int32, (width, width), 1)
    wide = jnp.concatenate([gram, jnp.where(row == column, 1.0, 0.0)], axis=1)
    n_groups = width // 8
    sublane = lax.broadcasted_iota(jnp.int32, (8, 2 * width), 0)
    if begin:
        wide = mid_ref[...]
    group = [wide[8 * g : 8 * g + 8, :] for g in range(n_groups)]
    step = 4
    for first in range(begin, end, step):
        g0 = first // 8
        live = range(g0, n_groups)
        columns = [
            {
                g: jnp.broadcast_to(group[g][:, first + k : first + k + 1], (8, 2 * width))
                for g in live
            }
            for k in range(step)
        ]
        for k in range(step):
            r = (first + k) % 8
            pivot_row = group[g0][r : r + 1, :]
            pivot = columns[k][g0][r : r + 1, :]
            inverse = 1.0 / pivot
            out_ref[first + k : first + k + 1, :] = pivot_row * lax.rsqrt(pivot)
            scaled_row = pivot_row * inverse
            heads = [columns[l][g0][r : r + 1, :] * inverse for l in range(k + 1, step)]
            for g in live:
                factor = columns[k][g]
                if g == g0:
                    factor = jnp.where(sublane > r, factor, 0.0)
                group[g] = group[g] - factor * scaled_row
                for l in range(k + 1, step):
                    columns[l][g] = columns[l][g] - factor * heads[l - k - 1]
    if end < width:
        for g in range(end // 8, n_groups):
            mid_ref[8 * g : 8 * g + 8, :] = group[g]


def write_upper(root_rows, wide_ref, upper_ref):
    width = upper_ref.shape[0]
    row = lax.broadcasted_iota(jnp.int32, (width, width), 0)
    column = lax.broadcasted_iota(jnp.int32, (width, width), 1)
    wide = wide_ref[...]
    upper_ref[...] = jnp.where(column >= row, wide[:, :width], 0.0) * (1.0 / root_rows)
    high, low = halves(wide[:, width:])
    return jnp.concatenate([high, high, low, low], axis=1)


def applied_inverse(stacked, values):
    high, low = halves(values)
    return jnp.dot(
        stacked,
        jnp.concatenate([high, low, high, low], axis=0),
        preferred_element_type=jnp.float32,
    )


def write_projection(root_rows, stacked, sums_ref, proj_ref, block):
    width = stacked.shape[0]
    start = block * LANES
    count = min(LANES, proj_ref.shape[1] - start)
    result = applied_inverse(stacked, sums_ref[block * width : (block + 1) * width, :])
    proj_ref[:, start : start + count] = (result * (1.0 / root_rows))[:, :count]


def write_basis(root_rows, stacked, panel_ref, basis_ref):
    for start in range(0, panel_ref.shape[1], BATCH):
        basis_ref[:, start : start + BATCH] = (
            applied_inverse(stacked, panel_ref[:, start : start + BATCH]) * root_rows
        )


def ordered_sum(own_ref, slots_ref, me, count):
    result = jnp.zeros(own_ref.shape, own_ref.dtype)
    for source in range(count):
        back = lax.rem(me - source + count, count)
        taken = slots_ref[lax.max(back - 1, 0)]
        result = result + jnp.where(back == 0, own_ref[...], taken)
    return result


def sum_kernel(
    n_gx,
    n_gy,
    panel_ref,
    following_ref,
    sums_ref,
    wide_ref,
    panel_vmem,
    rows_vmem,
    panel_turned,
    part,
    mid_ref,
    gram_own,
    gram_pair,
    gram_chip,
    gram_plane,
    gram_mid,
    gram_line,
    half_in,
    half_sum,
    quarter_in,
    quarter_sum,
    piece_in,
    total,
    load_panel_sem,
    load_sem,
    pair_sems,
    gram_plane_sems,
    gram_line_sems,
    half_sems,
    rs_plane_sems,
    rs_line_sems,
    ag_line_sems,
    ag_plane_sems,
    back_sems,
):
    width = panel_ref.shape[0]
    units = rows_vmem.shape[0] // width
    half_batches = rows_vmem.shape[0] // BATCH // 2
    batch_rows = BATCH // LANES * width
    half_rows = half_batches * batch_rows
    n_rings = n_gy // 2
    n_plane, n_line = 2 * n_rings, n_gx // 2
    quarter = half_rows // n_plane
    piece = quarter // n_line
    me_x, me_y = lax.axis_index("gx"), lax.axis_index("gy")
    core = lax.rem(me_y, 2)
    other = 1 - core
    in_plane = lax.rem(me_x, 2) * n_rings + me_y // 2
    in_line = me_x // 2
    sibling = (me_x, me_y + 1 - 2 * core)

    def plane_index(k):
        return lax.rem(in_plane + k, n_plane)

    def plane_device(k):
        index = plane_index(k)
        return (in_line * 2 + index // n_rings, lax.rem(index, n_rings) * 2 + core)

    def line_index(k):
        return lax.rem(in_line + k, n_line)

    def line_device(k):
        return (line_index(k) * 2 + lax.rem(me_x, 2), me_y)

    load_panel = pltpu.make_async_copy(panel_ref, panel_vmem, load_panel_sem)
    load_panel.start()

    @pl.loop(0, units)
    def _(step):
        unit = lax.rem(step + other * (units // 2), units)

        def load(source):
            pltpu.make_async_copy(
                source, rows_vmem.at[pl.ds(unit * width, width)], load_sem.at[unit]
            ).start()

        @pl.when(unit == units - 1)
        def _():
            load(panel_ref)

        @pl.when(unit != units - 1)
        def _():
            load(following_ref.at[pl.ds(unit * width, width)])

    barrier = pltpu.get_barrier_semaphore()

    def greet(device):
        pl.semaphore_signal(barrier, inc=1, device_id=device, device_id_type=MESH)

    greet(sibling)
    pl.loop(1, n_plane)(lambda k: greet(plane_device(k)))
    pl.loop(1, n_line)(lambda k: greet(line_device(k)))
    n_signals = n_plane + n_line - 1

    load_panel.wait()
    panel = panel_vmem[...]
    high = panel.astype(jnp.bfloat16).astype(jnp.float32)
    split = jnp.concatenate([high, panel - high], axis=0)
    panel_turned[...] = split.T.astype(jnp.bfloat16)
    quads = product(split.astype(jnp.bfloat16), panel_turned[...])
    pair = quads[:width] + quads[width:]
    gram = pair[:, :width] + pair[:, width:]
    gram_own[...] = jnp.concatenate([gram[: width // 2], gram[width // 2 :]], axis=1)

    pl.semaphore_wait(barrier, n_signals)

    def remote(source, target, sems, k, device):
        return pltpu.make_async_remote_copy(
            src_ref=source,
            dst_ref=target,
            send_sem=sems.at[0, k],
            recv_sem=sems.at[1, k],
            device_id=device,
            device_id_type=MESH,
        )

    def pair_copy():
        return remote(gram_own, gram_pair, pair_sems, 0, sibling)

    def gram_plane_copy(k):
        return remote(gram_chip, gram_plane.at[k - 1], gram_plane_sems, k - 1, plane_device(k))

    def gram_line_copy(k):
        return remote(gram_mid, gram_line.at[k - 1], gram_line_sems, k - 1, line_device(k))

    def half_copy():
        source = part.at[pl.ds(other * half_rows, half_rows)]
        return remote(source, half_in, half_sems, 0, sibling)

    def scatter_plane_copy(k):
        source = half_sum.at[pl.ds(plane_index(k) * quarter, quarter)]
        return remote(source, quarter_in.at[k - 1], rs_plane_sems, k - 1, plane_device(k))

    def scatter_line_copy(k):
        source = quarter_sum.at[pl.ds(line_index(k) * piece, piece)]
        return remote(source, piece_in.at[k - 1], rs_line_sems, k - 1, line_device(k))

    own_quarter = core * half_rows + in_plane * quarter
    own_piece = own_quarter + in_line * piece

    def gather_line_copy(k):
        block = total.at[pl.ds(own_piece, piece)]
        return remote(block, block, ag_line_sems, k - 1, line_device(k))

    def gather_plane_copy(k):
        block = total.at[pl.ds(own_quarter, quarter)]
        return remote(block, block, ag_plane_sems, k - 1, plane_device(k))

    def back_copy():
        block = total.at[pl.ds(core * half_rows, half_rows)]
        return remote(block, block, back_sems, 0, sibling)

    def start_all(copy, count):
        pl.loop(1, count)(lambda k: copy(k).start())

    def receive_all(copy, count):
        pl.loop(1, count)(lambda k: copy(k).wait_recv())

    def sent_all(copy, count):
        pl.loop(1, count)(lambda k: copy(k).wait_send())

    pair_copy().start()

    @pl.loop(0, 2 * half_batches)
    def _(step):
        half = lax.rem(other + step // half_batches, 2)
        index = half * half_batches + lax.rem(step, half_batches)
        for k in range(BATCH // width):
            unit = index * (BATCH // width) + k
            pltpu.make_async_copy(
                panel_ref, rows_vmem.at[pl.ds(unit * width, width)], load_sem.at[unit]
            ).wait()
        pair = jnp.zeros((BATCH, 2 * width), jnp.float32)
        for start in range(0, rows_vmem.shape[1], CELLS):
            rows = rows_vmem[pl.ds(index * BATCH, BATCH), start : start + CELLS]
            quads = product(
                jnp.concatenate(halves(rows), axis=0), panel_turned[start : start + CELLS, :]
            )
            pair = pair + (quads[:BATCH] + quads[BATCH:])
        for k in range(BATCH // LANES):
            turned = pair[k * LANES : (k + 1) * LANES].T
            part[pl.ds(index * batch_rows + k * width, width), :] = turned[:width] + turned[width:]

        @pl.when(step == 0)
        def _():
            pair_copy().wait_recv()
            gram_chip[...] = gram_own[...] + gram_pair[...]
            start_all(gram_plane_copy, n_plane)

        @pl.when(step == half_batches - 1)
        def _():
            half_copy().start()

        @pl.when(step == half_batches)
        def _():
            receive_all(gram_plane_copy, n_plane)
            gram_mid[...] = ordered_sum(gram_chip, gram_plane, in_plane, n_plane)
            start_all(gram_line_copy, n_line)

    half_copy().wait_recv()
    half_sum[...] = part[pl.ds(core * half_rows, half_rows), :] + half_in[...]
    start_all(scatter_plane_copy, n_plane)

    receive_all(gram_line_copy, n_line)
    packed = ordered_sum(gram_mid, gram_line, in_line, n_line)
    gram = jnp.concatenate([packed[:, :width], packed[:, width:]], axis=0)
    columns = width // 2
    eliminate(gram, wide_ref, mid_ref, 0, columns)

    receive_all(scatter_plane_copy, n_plane)
    summed = half_sum[pl.ds(in_plane * quarter, quarter), :]
    for k in range(n_plane - 1):
        summed = summed + quarter_in[k]
    quarter_sum[...] = summed
    start_all(scatter_line_copy, n_line)

    eliminate(gram, wide_ref, mid_ref, columns, width)

    receive_all(scatter_line_copy, n_line)
    summed = quarter_sum[pl.ds(in_line * piece, piece), :]
    for k in range(n_line - 1):
        summed = summed + piece_in[k]
    total[pl.ds(own_piece, piece), :] = summed
    start_all(gather_line_copy, n_line)
    pair_copy().wait_send()
    half_copy().wait_send()
    sent_all(gram_plane_copy, n_plane)
    sent_all(gram_line_copy, n_line)
    sent_all(scatter_plane_copy, n_plane)
    sent_all(scatter_line_copy, n_line)
    receive_all(gather_line_copy, n_line)
    start_all(gather_plane_copy, n_plane)
    sent_all(gather_line_copy, n_line)
    receive_all(gather_plane_copy, n_plane)
    back_copy().start()
    sent_all(gather_plane_copy, n_plane)
    back_copy().wait_recv()
    sums_ref[...] = total[...]
    back_copy().wait_send()


def exchanged(panel, following, n_gx, n_gy):
    width, cells = panel.shape
    rows = width + following.shape[0]
    all_rows = rows // LANES * width
    half_rows = all_rows // 2
    n_plane, n_line = n_gy, n_gx // 2
    quarter = half_rows // n_plane
    piece = quarter // n_line
    gram_block = (width // 2, 2 * width)
    dma = pltpu.SemaphoreType.DMA
    f32 = jnp.float32
    return pl.pallas_call(
        functools.partial(sum_kernel, n_gx, n_gy),
        out_shape=(
            jax.ShapeDtypeStruct((all_rows, LANES), f32),
            jax.ShapeDtypeStruct((width, 2 * width), f32),
        ),
        in_specs=[pl.BlockSpec(memory_space=pltpu.HBM)] * 2,
        out_specs=(
            pl.BlockSpec(memory_space=pltpu.VMEM),
            pl.BlockSpec(memory_space=pltpu.VMEM),
        ),
        scratch_shapes=[
            pltpu.VMEM((width, cells), f32),
            pltpu.VMEM((rows, cells), f32),
            pltpu.VMEM((cells, 2 * width), jnp.bfloat16),
            pltpu.VMEM((all_rows, LANES), f32),
            pltpu.VMEM((width, 2 * width), f32),
            pltpu.VMEM(gram_block, f32),
            pltpu.VMEM(gram_block, f32),
            pltpu.VMEM(gram_block, f32),
            pltpu.VMEM((n_plane - 1,) + gram_block, f32),
            pltpu.VMEM(gram_block, f32),
            pltpu.VMEM((n_line - 1,) + gram_block, f32),
            pltpu.VMEM((half_rows, LANES), f32),
            pltpu.VMEM((half_rows, LANES), f32),
            pltpu.VMEM((n_plane - 1, quarter, LANES), f32),
            pltpu.VMEM((quarter, LANES), f32),
            pltpu.VMEM((n_line - 1, piece, LANES), f32),
            pltpu.VMEM((all_rows, LANES), f32),
            dma,
            dma((rows // width,)),
            dma((2, 1)),
            dma((2, n_plane - 1)),
            dma((2, n_line - 1)),
            dma((2, 1)),
            dma((2, n_plane - 1)),
            dma((2, n_line - 1)),
            dma((2, n_line - 1)),
            dma((2, n_plane - 1)),
            dma((2, 1)),
        ],
        compiler_params=pltpu.CompilerParams(
            collective_id=0, has_side_effects=True, vmem_limit_bytes=56 * 2**20
        ),
        name="sum_and_factor",
    )(panel, following)


def apply_kernel(root_rows, sums_ref, wide_ref, panel_ref, basis_ref, upper_ref, proj_ref):
    stacked = write_upper(root_rows, wide_ref, upper_ref)
    for block in range(sums_ref.shape[0] // panel_ref.shape[0]):
        write_projection(root_rows, stacked, sums_ref, proj_ref, block)
    write_basis(root_rows, stacked, panel_ref, basis_ref)


def applied(sums, wide, panel, next_count, root_rows):
    width, cells = panel.shape
    f32 = jnp.float32
    return pl.pallas_call(
        functools.partial(apply_kernel, root_rows),
        out_shape=(
            jax.ShapeDtypeStruct((width, cells), f32),
            jax.ShapeDtypeStruct((width, width), f32),
            jax.ShapeDtypeStruct((width, next_count), f32),
        ),
        compiler_params=pltpu.CompilerParams(vmem_limit_bytes=60 * 2**20),
        name="apply_factor",
    )(sums, wide, panel)


def plain_sums(panel, following):
    precise = functools.partial(
        lax.dot_general,
        dimension_numbers=(((1,), (1,)), ((), ())),
        precision=lax.Precision.HIGHEST,
        preferred_element_type=jnp.float32,
    )
    width = panel.shape[0]
    cross = lax.psum(
        jnp.concatenate([precise(panel, following), precise(panel, panel)], axis=1), ("gx", "gy")
    )
    blocks = cross.shape[1] // LANES
    sums = cross.reshape(width, blocks, LANES).transpose(1, 0, 2).reshape(blocks * width, LANES)
    wide = pl.pallas_call(
        lambda gram_ref, wide_ref: eliminate(gram_ref[...], wide_ref, None, 0, width),
        out_shape=jax.ShapeDtypeStruct((width, 2 * width), jnp.float32),
        name="factor",
    )(cross[:, -width:])
    return sums, wide


def body(n_gx, n_gy, panel, following):
    width, cells = panel.shape
    root_rows = math.sqrt(cells * n_gx * n_gy)
    half_rows = (width + following.shape[0]) // LANES * width // 2
    if half_rows % (8 * (n_gx * n_gy // 2)) == 0:
        sums, wide = exchanged(panel, following, n_gx, n_gy)
    else:
        sums, wide = plain_sums(panel, following)
    return applied(sums, wide, panel, following.shape[0], root_rows)


def solution(mesh):
    return jax.shard_map(
        functools.partial(body, mesh.shape["gx"], mesh.shape["gy"]),
        mesh=mesh,
        in_specs=(P(None, ("gx", "gy")), P(None, ("gx", "gy"))),
        out_specs=(P(None, ("gx", "gy")), P(), P()),
        check_vma=False,
    )
```

```python
import functools
import math

import jax
import jax.numpy as jnp
from jax import lax
from jax.experimental import pallas as pl
from jax.experimental.pallas import tpu as pltpu
from jax.sharding import PartitionSpec as P

MESH = pl.DeviceIdType.MESH
LANES = 128
BATCH = 256
CELLS = 512


def halves(values):
    high = values.astype(jnp.bfloat16)
    return high, (values - high.astype(jnp.float32)).astype(jnp.bfloat16)


def product(left, right):
    return jnp.dot(left, right, preferred_element_type=jnp.float32)


def eliminate(gram, out_ref):
    width = gram.shape[0]
    row = lax.broadcasted_iota(jnp.int32, (width, width), 0)
    column = lax.broadcasted_iota(jnp.int32, (width, width), 1)
    wide = jnp.concatenate([gram, jnp.where(row == column, 1.0, 0.0)], axis=1)
    n_groups = width // 8
    sublane = lax.broadcasted_iota(jnp.int32, (8, 2 * width), 0)
    group = [wide[8 * g : 8 * g + 8, :] for g in range(n_groups)]
    step = 4
    for first in range(0, width, step):
        g0 = first // 8
        live = range(g0, n_groups)
        columns = [
            {
                g: jnp.broadcast_to(group[g][:, first + k : first + k + 1], (8, 2 * width))
                for g in live
            }
            for k in range(step)
        ]
        for k in range(step):
            r = (first + k) % 8
            pivot_row = group[g0][r : r + 1, :]
            pivot = columns[k][g0][r : r + 1, :]
            inverse = 1.0 / pivot
            out_ref[first + k : first + k + 1, :] = pivot_row * lax.rsqrt(pivot)
            scaled_row = pivot_row * inverse
            heads = [columns[l][g0][r : r + 1, :] * inverse for l in range(k + 1, step)]
            for g in live:
                factor = columns[k][g]
                if g == g0:
                    factor = jnp.where(sublane > r, factor, 0.0)
                group[g] = group[g] - factor * scaled_row
                for l in range(k + 1, step):
                    columns[l][g] = columns[l][g] - factor * heads[l - k - 1]


def write_upper(root_rows, wide_ref, upper_ref):
    width = upper_ref.shape[0]
    row = lax.broadcasted_iota(jnp.int32, (width, width), 0)
    column = lax.broadcasted_iota(jnp.int32, (width, width), 1)
    wide = wide_ref[...]
    upper_ref[...] = jnp.where(column >= row, wide[:, :width], 0.0) * (1.0 / root_rows)
    high, low = halves(wide[:, width:])
    return jnp.concatenate([high, high, low, low], axis=1)


def applied_inverse(stacked, values):
    high, low = halves(values)
    return jnp.dot(
        stacked,
        jnp.concatenate([high, low, high, low], axis=0),
        preferred_element_type=jnp.float32,
    )


def write_projection(root_rows, stacked, sums_ref, proj_ref, block):
    width = stacked.shape[0]
    start = block * LANES
    count = min(LANES, proj_ref.shape[1] - start)
    result = applied_inverse(stacked, sums_ref[block * width : (block + 1) * width, :])
    proj_ref[:, start : start + count] = (result * (1.0 / root_rows))[:, :count]


def write_basis(root_rows, stacked, panel_ref, basis_ref):
    for start in range(0, panel_ref.shape[1], BATCH):
        basis_ref[:, start : start + BATCH] = (
            applied_inverse(stacked, panel_ref[:, start : start + BATCH]) * root_rows
        )


def ordered_sum(own_ref, slots_ref, me, count):
    result = jnp.zeros(own_ref.shape, own_ref.dtype)
    for source in range(count):
        back = lax.rem(me - source + count, count)
        taken = slots_ref[lax.max(back - 1, 0)]
        result = result + jnp.where(back == 0, own_ref[...], taken)
    return result


def sum_kernel(
    n_gx,
    n_gy,
    panel_ref,
    following_ref,
    sums_ref,
    wide_ref,
    panel_vmem,
    rows_vmem,
    panel_turned,
    part,
    gram_own,
    gram_gy,
    gram_mid,
    gram_gx,
    half_in,
    half_sum,
    piece_in,
    total,
    load_panel_sem,
    load_sem,
    gy_send,
    gy_recv,
    gx_send,
    gx_recv,
    half_send,
    half_recv,
    rs_send,
    rs_recv,
    ag_send,
    ag_recv,
    back_send,
    back_recv,
):
    width = panel_ref.shape[0]
    units = rows_vmem.shape[0] // width
    half_batches = rows_vmem.shape[0] // BATCH // 2
    batch_rows = BATCH // LANES * width
    half_rows = half_batches * batch_rows
    n_chips = n_gx * n_gy // 2
    piece = half_rows // n_chips
    me_x, me_y = lax.axis_index("gx"), lax.axis_index("gy")
    core = lax.rem(me_y, 2)
    other = 1 - core
    chip = me_x * (n_gy // 2) + me_y // 2
    sibling = (me_x, me_y + 1 - 2 * core)

    def chip_device(index):
        return (index // (n_gy // 2), lax.rem(index, n_gy // 2) * 2 + core)

    load_panel = pltpu.make_async_copy(panel_ref, panel_vmem, load_panel_sem)
    load_panel.start()

    @pl.loop(0, units)
    def _(step):
        unit = lax.rem(step + other * (units // 2), units)

        def load(source):
            pltpu.make_async_copy(
                source, rows_vmem.at[pl.ds(unit * width, width)], load_sem.at[unit]
            ).start()

        @pl.when(unit == units - 1)
        def _():
            load(panel_ref)

        @pl.when(unit != units - 1)
        def _():
            load(following_ref.at[pl.ds(unit * width, width)])

    barrier = pltpu.get_barrier_semaphore()

    @pl.loop(1, n_chips)
    def _(k):
        pl.semaphore_signal(
            barrier, inc=1, device_id=chip_device(lax.rem(chip + k, n_chips)), device_id_type=MESH
        )

    for k in range(1, n_gy, 2):
        pl.semaphore_signal(
            barrier, inc=1, device_id=(me_x, lax.rem(me_y + k, n_gy)), device_id_type=MESH
        )
    n_signals = n_chips - 1 + n_gy // 2

    load_panel.wait()
    panel = panel_vmem[...]
    high = panel.astype(jnp.bfloat16).astype(jnp.float32)
    split = jnp.concatenate([high, panel - high], axis=0)
    panel_turned[...] = split.T.astype(jnp.bfloat16)
    quads = product(split.astype(jnp.bfloat16), panel_turned[...])
    pair = quads[:width] + quads[width:]
    gram = pair[:, :width] + pair[:, width:]
    gram_own[...] = jnp.concatenate([gram[: width // 2], gram[width // 2 :]], axis=1)

    pl.semaphore_wait(barrier, n_signals)

    def gy_copy(k):
        return pltpu.make_async_remote_copy(
            src_ref=gram_own,
            dst_ref=gram_gy.at[k - 1],
            send_sem=gy_send.at[k - 1],
            recv_sem=gy_recv.at[k - 1],
            device_id=(me_x, lax.rem(me_y + k, n_gy)),
            device_id_type=MESH,
        )

    def gx_copy(k):
        return pltpu.make_async_remote_copy(
            src_ref=gram_mid,
            dst_ref=gram_gx.at[k - 1],
            send_sem=gx_send.at[k - 1],
            recv_sem=gx_recv.at[k - 1],
            device_id=(lax.rem(me_x + k, n_gx), me_y),
            device_id_type=MESH,
        )

    def half_copy():
        return pltpu.make_async_remote_copy(
            src_ref=part.at[pl.ds(other * half_rows, half_rows)],
            dst_ref=half_in,
            send_sem=half_send,
            recv_sem=half_recv,
            device_id=sibling,
            device_id_type=MESH,
        )

    def scatter_copy(k):
        to = lax.rem(chip + k, n_chips)
        return pltpu.make_async_remote_copy(
            src_ref=half_sum.at[pl.ds(to * piece, piece)],
            dst_ref=piece_in.at[k - 1],
            send_sem=rs_send.at[k - 1],
            recv_sem=rs_recv.at[k - 1],
            device_id=chip_device(to),
            device_id_type=MESH,
        )

    own_start = core * half_rows + chip * piece

    def gather_copy(k):
        return pltpu.make_async_remote_copy(
            src_ref=total.at[pl.ds(own_start, piece)],
            dst_ref=total.at[pl.ds(own_start, piece)],
            send_sem=ag_send.at[k - 1],
            recv_sem=ag_recv.at[k - 1],
            device_id=chip_device(lax.rem(chip + k, n_chips)),
            device_id_type=MESH,
        )

    def back_copy(k):
        start = core * half_rows + lax.rem(chip - k + n_chips, n_chips) * piece
        return pltpu.make_async_remote_copy(
            src_ref=total.at[pl.ds(start, piece)],
            dst_ref=total.at[pl.ds(start, piece)],
            send_sem=back_send.at[k],
            recv_sem=back_recv.at[k],
            device_id=sibling,
            device_id_type=MESH,
        )

    def start_all(copy, count):
        pl.loop(1, count)(lambda k: copy(k).start())

    def receive_all(copy, count):
        pl.loop(1, count)(lambda k: copy(k).wait_recv())

    def sent_all(copy, count):
        pl.loop(1, count)(lambda k: copy(k).wait_send())

    start_all(gy_copy, n_gy)

    @pl.loop(0, 2 * half_batches)
    def _(step):
        half = lax.rem(other + step // half_batches, 2)
        index = half * half_batches + lax.rem(step, half_batches)
        for k in range(BATCH // width):
            unit = index * (BATCH // width) + k
            pltpu.make_async_copy(
                panel_ref, rows_vmem.at[pl.ds(unit * width, width)], load_sem.at[unit]
            ).wait()
        pair = jnp.zeros((BATCH, 2 * width), jnp.float32)
        for start in range(0, rows_vmem.shape[1], CELLS):
            rows = rows_vmem[pl.ds(index * BATCH, BATCH), start : start + CELLS]
            quads = product(
                jnp.concatenate(halves(rows), axis=0), panel_turned[start : start + CELLS, :]
            )
            pair = pair + (quads[:BATCH] + quads[BATCH:])
        for k in range(BATCH // LANES):
            turned = pair[k * LANES : (k + 1) * LANES].T
            part[pl.ds(index * batch_rows + k * width, width), :] = turned[:width] + turned[width:]

        @pl.when(step == half_batches - 1)
        def _():
            half_copy().start()
            receive_all(gy_copy, n_gy)
            gram_mid[...] = ordered_sum(gram_own, gram_gy, me_y, n_gy)
            start_all(gx_copy, n_gx)

    half_copy().wait_recv()
    half_sum[...] = part[pl.ds(core * half_rows, half_rows), :] + half_in[...]
    start_all(scatter_copy, n_chips)

    receive_all(gx_copy, n_gx)
    packed = ordered_sum(gram_mid, gram_gx, me_x, n_gx)
    eliminate(jnp.concatenate([packed[:, :width], packed[:, width:]], axis=0), wide_ref)

    receive_all(scatter_copy, n_chips)
    own = half_sum[pl.ds(chip * piece, piece), :]
    for k in range(n_chips - 1):
        own = own + piece_in[k]
    total[pl.ds(own_start, piece), :] = own
    start_all(gather_copy, n_chips)
    back_copy(0).start()

    @pl.loop(1, n_chips)
    def _(k):
        gather_copy(k).wait_recv()
        back_copy(k).start()

    sent_all(gy_copy, n_gy)
    sent_all(gx_copy, n_gx)
    half_copy().wait_send()
    sent_all(scatter_copy, n_chips)
    sent_all(gather_copy, n_chips)

    @pl.loop(0, n_chips)
    def _(k):
        back_copy(k).wait_recv()
        back_copy(k).wait_send()

    sums_ref[...] = total[...]


def exchanged(panel, following, n_gx, n_gy):
    width, cells = panel.shape
    rows = width + following.shape[0]
    all_rows = rows // LANES * width
    half_rows = all_rows // 2
    n_chips = n_gx * n_gy // 2
    piece = half_rows // n_chips
    gram_block = (width // 2, 2 * width)
    dma = pltpu.SemaphoreType.DMA
    f32 = jnp.float32
    return pl.pallas_call(
        functools.partial(sum_kernel, n_gx, n_gy),
        out_shape=(
            jax.ShapeDtypeStruct((all_rows, LANES), f32),
            jax.ShapeDtypeStruct((width, 2 * width), f32),
        ),
        in_specs=[pl.BlockSpec(memory_space=pltpu.HBM)] * 2,
        out_specs=(
            pl.BlockSpec(memory_space=pltpu.VMEM),
            pl.BlockSpec(memory_space=pltpu.VMEM),
        ),
        scratch_shapes=[
            pltpu.VMEM((width, cells), f32),
            pltpu.VMEM((rows, cells), f32),
            pltpu.VMEM((cells, 2 * width), jnp.bfloat16),
            pltpu.VMEM((all_rows, LANES), f32),
            pltpu.VMEM(gram_block, f32),
            pltpu.VMEM((n_gy - 1,) + gram_block, f32),
            pltpu.VMEM(gram_block, f32),
            pltpu.VMEM((n_gx - 1,) + gram_block, f32),
            pltpu.VMEM((half_rows, LANES), f32),
            pltpu.VMEM((half_rows, LANES), f32),
            pltpu.VMEM((n_chips - 1, piece, LANES), f32),
            pltpu.VMEM((all_rows, LANES), f32),
            dma,
            dma((rows // width,)),
            dma((n_gy - 1,)),
            dma((n_gy - 1,)),
            dma((n_gx - 1,)),
            dma((n_gx - 1,)),
            dma,
            dma,
            dma((n_chips - 1,)),
            dma((n_chips - 1,)),
            dma((n_chips - 1,)),
            dma((n_chips - 1,)),
            dma((n_chips,)),
            dma((n_chips,)),
        ],
        compiler_params=pltpu.CompilerParams(
            collective_id=0, has_side_effects=True, vmem_limit_bytes=107 * 2**19
        ),
        name="sum_and_factor",
    )(panel, following)


def apply_kernel(root_rows, sums_ref, wide_ref, panel_ref, basis_ref, upper_ref, proj_ref):
    stacked = write_upper(root_rows, wide_ref, upper_ref)
    for block in range(sums_ref.shape[0] // panel_ref.shape[0]):
        write_projection(root_rows, stacked, sums_ref, proj_ref, block)
    write_basis(root_rows, stacked, panel_ref, basis_ref)


def applied(sums, wide, panel, next_count, root_rows):
    width, cells = panel.shape
    f32 = jnp.float32
    return pl.pallas_call(
        functools.partial(apply_kernel, root_rows),
        out_shape=(
            jax.ShapeDtypeStruct((width, cells), f32),
            jax.ShapeDtypeStruct((width, width), f32),
            jax.ShapeDtypeStruct((width, next_count), f32),
        ),
        compiler_params=pltpu.CompilerParams(vmem_limit_bytes=16 * 2**20),
        name="apply_factor",
    )(sums, wide, panel)


def plain_sums(panel, following):
    precise = functools.partial(
        lax.dot_general,
        dimension_numbers=(((1,), (1,)), ((), ())),
        precision=lax.Precision.HIGHEST,
        preferred_element_type=jnp.float32,
    )
    width = panel.shape[0]
    cross = lax.psum(
        jnp.concatenate([precise(panel, following), precise(panel, panel)], axis=1), ("gx", "gy")
    )
    blocks = cross.shape[1] // LANES
    sums = cross.reshape(width, blocks, LANES).transpose(1, 0, 2).reshape(blocks * width, LANES)
    wide = pl.pallas_call(
        lambda gram_ref, wide_ref: eliminate(gram_ref[...], wide_ref),
        out_shape=jax.ShapeDtypeStruct((width, 2 * width), jnp.float32),
        name="factor",
    )(cross[:, -width:])
    return sums, wide


def body(n_gx, n_gy, panel, following):
    width, cells = panel.shape
    root_rows = math.sqrt(cells * n_gx * n_gy)
    half_rows = (width + following.shape[0]) // LANES * width // 2
    if half_rows % (8 * (n_gx * n_gy // 2)) == 0:
        sums, wide = exchanged(panel, following, n_gx, n_gy)
    else:
        sums, wide = plain_sums(panel, following)
    return applied(sums, wide, panel, following.shape[0], root_rows)


def solution(mesh):
    return jax.shard_map(
        functools.partial(body, mesh.shape["gx"], mesh.shape["gy"]),
        mesh=mesh,
        in_specs=(P(None, ("gx", "gy")), P(None, ("gx", "gy"))),
        out_specs=(P(None, ("gx", "gy")), P(), P()),
        check_vma=False,
    )
```

```python
import functools
import math

import jax
import jax.numpy as jnp
from jax import lax
from jax.experimental import pallas as pl
from jax.experimental.pallas import tpu as pltpu
from jax.sharding import PartitionSpec as P

MESH = pl.DeviceIdType.MESH
LANES = 128
BATCH = 256
CELLS = 512


def halves(values):
    high = values.astype(jnp.bfloat16)
    return high, (values - high.astype(jnp.float32)).astype(jnp.bfloat16)


def product(left, right):
    return jnp.dot(left, right, preferred_element_type=jnp.float32)


def eliminate(gram, out_ref):
    width = gram.shape[0]
    row = lax.broadcasted_iota(jnp.int32, (width, width), 0)
    column = lax.broadcasted_iota(jnp.int32, (width, width), 1)
    wide = jnp.concatenate([gram, jnp.where(row == column, 1.0, 0.0)], axis=1)
    n_groups = width // 8
    sublane = lax.broadcasted_iota(jnp.int32, (8, 2 * width), 0)
    group = [wide[8 * g : 8 * g + 8, :] for g in range(n_groups)]
    step = 4
    for first in range(0, width, step):
        g0 = first // 8
        live = range(g0, n_groups)
        columns = [
            {
                g: jnp.broadcast_to(group[g][:, first + k : first + k + 1], (8, 2 * width))
                for g in live
            }
            for k in range(step)
        ]
        for k in range(step):
            r = (first + k) % 8
            pivot_row = group[g0][r : r + 1, :]
            pivot = columns[k][g0][r : r + 1, :]
            inverse = 1.0 / pivot
            out_ref[first + k : first + k + 1, :] = pivot_row * lax.rsqrt(pivot)
            scaled_row = pivot_row * inverse
            heads = [columns[l][g0][r : r + 1, :] * inverse for l in range(k + 1, step)]
            for g in live:
                factor = columns[k][g]
                if g == g0:
                    factor = jnp.where(sublane > r, factor, 0.0)
                group[g] = group[g] - factor * scaled_row
                for l in range(k + 1, step):
                    columns[l][g] = columns[l][g] - factor * heads[l - k - 1]


def write_upper(root_rows, wide_ref, upper_ref):
    width = upper_ref.shape[0]
    row = lax.broadcasted_iota(jnp.int32, (width, width), 0)
    column = lax.broadcasted_iota(jnp.int32, (width, width), 1)
    wide = wide_ref[...]
    upper_ref[...] = jnp.where(column >= row, wide[:, :width], 0.0) * (1.0 / root_rows)
    high, low = halves(wide[:, width:])
    return jnp.concatenate([high, high, low, low], axis=1)


def applied_inverse(stacked, values):
    high, low = halves(values)
    return jnp.dot(
        stacked,
        jnp.concatenate([high, low, high, low], axis=0),
        preferred_element_type=jnp.float32,
    )


def write_projection(root_rows, stacked, sums_ref, proj_ref, block):
    width = stacked.shape[0]
    start = block * LANES
    count = min(LANES, proj_ref.shape[1] - start)
    result = applied_inverse(stacked, sums_ref[block * width : (block + 1) * width, :])
    proj_ref[:, start : start + count] = (result * (1.0 / root_rows))[:, :count]


def write_basis(root_rows, stacked, panel_ref, basis_ref):
    for start in range(0, panel_ref.shape[1], BATCH):
        basis_ref[:, start : start + BATCH] = (
            applied_inverse(stacked, panel_ref[:, start : start + BATCH]) * root_rows
        )


def ordered_sum(own_ref, slots_ref, me, count):
    result = jnp.zeros(own_ref.shape, own_ref.dtype)
    for source in range(count):
        back = lax.rem(me - source + count, count)
        taken = slots_ref[lax.max(back - 1, 0)]
        result = result + jnp.where(back == 0, own_ref[...], taken)
    return result


def sum_kernel(
    n_gx,
    n_gy,
    panel_ref,
    following_ref,
    sums_ref,
    wide_ref,
    panel_vmem,
    rows_vmem,
    panel_turned,
    part,
    gram_own,
    gram_gy,
    gram_mid,
    gram_gx,
    half_in,
    half_sum,
    piece_in,
    total,
    load_panel_sem,
    load_sem,
    gy_send,
    gy_recv,
    gx_send,
    gx_recv,
    half_send,
    half_recv,
    rs_send,
    rs_recv,
    ag_send,
    ag_recv,
    back_send,
    back_recv,
):
    width = panel_ref.shape[0]
    units = rows_vmem.shape[0] // width
    half_batches = rows_vmem.shape[0] // BATCH // 2
    batch_rows = BATCH // LANES * width
    half_rows = half_batches * batch_rows
    n_chips = n_gx * n_gy // 2
    piece = half_rows // n_chips
    me_x, me_y = lax.axis_index("gx"), lax.axis_index("gy")
    core = lax.rem(me_y, 2)
    other = 1 - core
    chip = me_x * (n_gy // 2) + me_y // 2
    sibling = (me_x, me_y + 1 - 2 * core)

    def chip_device(index):
        return (index // (n_gy // 2), lax.rem(index, n_gy // 2) * 2 + core)

    load_panel = pltpu.make_async_copy(panel_ref, panel_vmem, load_panel_sem)
    load_panel.start()

    @pl.loop(0, units)
    def _(step):
        unit = lax.rem(step + other * (units // 2), units)

        def load(source):
            pltpu.make_async_copy(
                source, rows_vmem.at[pl.ds(unit * width, width)], load_sem.at[unit]
            ).start()

        @pl.when(unit == units - 1)
        def _():
            load(panel_ref)

        @pl.when(unit != units - 1)
        def _():
            load(following_ref.at[pl.ds(unit * width, width)])

    barrier = pltpu.get_barrier_semaphore()

    @pl.loop(1, n_chips)
    def _(k):
        pl.semaphore_signal(
            barrier, inc=1, device_id=chip_device(lax.rem(chip + k, n_chips)), device_id_type=MESH
        )

    for k in range(1, n_gy, 2):
        pl.semaphore_signal(
            barrier, inc=1, device_id=(me_x, lax.rem(me_y + k, n_gy)), device_id_type=MESH
        )
    n_signals = n_chips - 1 + n_gy // 2

    load_panel.wait()
    panel = panel_vmem[...]
    high = panel.astype(jnp.bfloat16).astype(jnp.float32)
    split = jnp.concatenate([high, panel - high], axis=0)
    panel_turned[...] = split.T.astype(jnp.bfloat16)
    quads = product(split.astype(jnp.bfloat16), panel_turned[...])
    pair = quads[:width] + quads[width:]
    gram = pair[:, :width] + pair[:, width:]
    gram_own[...] = jnp.concatenate([gram[: width // 2], gram[width // 2 :]], axis=1)

    pl.semaphore_wait(barrier, n_signals)

    def gy_copy(k):
        return pltpu.make_async_remote_copy(
            src_ref=gram_own,
            dst_ref=gram_gy.at[k - 1],
            send_sem=gy_send.at[k - 1],
            recv_sem=gy_recv.at[k - 1],
            device_id=(me_x, lax.rem(me_y + k, n_gy)),
            device_id_type=MESH,
        )

    def gx_copy(k):
        return pltpu.make_async_remote_copy(
            src_ref=gram_mid,
            dst_ref=gram_gx.at[k - 1],
            send_sem=gx_send.at[k - 1],
            recv_sem=gx_recv.at[k - 1],
            device_id=(lax.rem(me_x + k, n_gx), me_y),
            device_id_type=MESH,
        )

    def half_copy():
        return pltpu.make_async_remote_copy(
            src_ref=part.at[pl.ds(other * half_rows, half_rows)],
            dst_ref=half_in,
            send_sem=half_send,
            recv_sem=half_recv,
            device_id=sibling,
            device_id_type=MESH,
        )

    def scatter_copy(k):
        to = lax.rem(chip + k, n_chips)
        return pltpu.make_async_remote_copy(
            src_ref=half_sum.at[pl.ds(to * piece, piece)],
            dst_ref=piece_in.at[k - 1],
            send_sem=rs_send.at[k - 1],
            recv_sem=rs_recv.at[k - 1],
            device_id=chip_device(to),
            device_id_type=MESH,
        )

    own_start = core * half_rows + chip * piece

    def gather_copy(k):
        return pltpu.make_async_remote_copy(
            src_ref=total.at[pl.ds(own_start, piece)],
            dst_ref=total.at[pl.ds(own_start, piece)],
            send_sem=ag_send.at[k - 1],
            recv_sem=ag_recv.at[k - 1],
            device_id=chip_device(lax.rem(chip + k, n_chips)),
            device_id_type=MESH,
        )

    def back_copy(k):
        start = core * half_rows + lax.rem(chip - k + n_chips, n_chips) * piece
        return pltpu.make_async_remote_copy(
            src_ref=total.at[pl.ds(start, piece)],
            dst_ref=total.at[pl.ds(start, piece)],
            send_sem=back_send.at[k],
            recv_sem=back_recv.at[k],
            device_id=sibling,
            device_id_type=MESH,
        )

    def start_all(copy, count):
        pl.loop(1, count)(lambda k: copy(k).start())

    def turned_order(k):
        return lax.rem(k + n_chips // 2 - 2, n_chips - 1) + 1

    def far_first(copy):
        pl.loop(1, n_chips)(lambda k: copy(turned_order(k)).start())

    def receive_all(copy, count):
        pl.loop(1, count)(lambda k: copy(k).wait_recv())

    def sent_all(copy, count):
        pl.loop(1, count)(lambda k: copy(k).wait_send())

    start_all(gy_copy, n_gy)

    @pl.loop(0, 2 * half_batches)
    def _(step):
        half = lax.rem(other + step // half_batches, 2)
        index = half * half_batches + lax.rem(step, half_batches)
        for k in range(BATCH // width):
            unit = index * (BATCH // width) + k
            pltpu.make_async_copy(
                panel_ref, rows_vmem.at[pl.ds(unit * width, width)], load_sem.at[unit]
            ).wait()
        pair = jnp.zeros((BATCH, 2 * width), jnp.float32)
        for start in range(0, rows_vmem.shape[1], CELLS):
            rows = rows_vmem[pl.ds(index * BATCH, BATCH), start : start + CELLS]
            quads = product(
                jnp.concatenate(halves(rows), axis=0), panel_turned[start : start + CELLS, :]
            )
            pair = pair + (quads[:BATCH] + quads[BATCH:])
        for k in range(BATCH // LANES):
            turned = pair[k * LANES : (k + 1) * LANES].T
            part[pl.ds(index * batch_rows + k * width, width), :] = turned[:width] + turned[width:]

        @pl.when(step == half_batches - 1)
        def _():
            half_copy().start()
            receive_all(gy_copy, n_gy)
            gram_mid[...] = ordered_sum(gram_own, gram_gy, me_y, n_gy)
            start_all(gx_copy, n_gx)

    half_copy().wait_recv()
    half_sum[...] = part[pl.ds(core * half_rows, half_rows), :] + half_in[...]
    far_first(scatter_copy)

    receive_all(gx_copy, n_gx)
    packed = ordered_sum(gram_mid, gram_gx, me_x, n_gx)
    eliminate(jnp.concatenate([packed[:, :width], packed[:, width:]], axis=0), wide_ref)

    receive_all(scatter_copy, n_chips)
    own = half_sum[pl.ds(chip * piece, piece), :]
    for k in range(n_chips - 1):
        own = own + piece_in[k]
    total[pl.ds(own_start, piece), :] = own
    far_first(gather_copy)
    back_copy(0).start()

    @pl.loop(1, n_chips)
    def _(k):
        gather_copy(turned_order(k)).wait_recv()
        back_copy(turned_order(k)).start()

    sent_all(gy_copy, n_gy)
    sent_all(gx_copy, n_gx)
    half_copy().wait_send()
    sent_all(scatter_copy, n_chips)
    sent_all(gather_copy, n_chips)

    @pl.loop(0, n_chips)
    def _(k):
        back_copy(k).wait_recv()
        back_copy(k).wait_send()

    sums_ref[...] = total[...]


def exchanged(panel, following, n_gx, n_gy):
    width, cells = panel.shape
    rows = width + following.shape[0]
    all_rows = rows // LANES * width
    half_rows = all_rows // 2
    n_chips = n_gx * n_gy // 2
    piece = half_rows // n_chips
    gram_block = (width // 2, 2 * width)
    dma = pltpu.SemaphoreType.DMA
    f32 = jnp.float32
    return pl.pallas_call(
        functools.partial(sum_kernel, n_gx, n_gy),
        out_shape=(
            jax.ShapeDtypeStruct((all_rows, LANES), f32),
            jax.ShapeDtypeStruct((width, 2 * width), f32),
        ),
        in_specs=[pl.BlockSpec(memory_space=pltpu.HBM)] * 2,
        out_specs=(
            pl.BlockSpec(memory_space=pltpu.VMEM),
            pl.BlockSpec(memory_space=pltpu.VMEM),
        ),
        scratch_shapes=[
            pltpu.VMEM((width, cells), f32),
            pltpu.VMEM((rows, cells), f32),
            pltpu.VMEM((cells, 2 * width), jnp.bfloat16),
            pltpu.VMEM((all_rows, LANES), f32),
            pltpu.VMEM(gram_block, f32),
            pltpu.VMEM((n_gy - 1,) + gram_block, f32),
            pltpu.VMEM(gram_block, f32),
            pltpu.VMEM((n_gx - 1,) + gram_block, f32),
            pltpu.VMEM((half_rows, LANES), f32),
            pltpu.VMEM((half_rows, LANES), f32),
            pltpu.VMEM((n_chips - 1, piece, LANES), f32),
            pltpu.VMEM((all_rows, LANES), f32),
            dma,
            dma((rows // width,)),
            dma((n_gy - 1,)),
            dma((n_gy - 1,)),
            dma((n_gx - 1,)),
            dma((n_gx - 1,)),
            dma,
            dma,
            dma((n_chips - 1,)),
            dma((n_chips - 1,)),
            dma((n_chips - 1,)),
            dma((n_chips - 1,)),
            dma((n_chips,)),
            dma((n_chips,)),
        ],
        compiler_params=pltpu.CompilerParams(
            collective_id=0, has_side_effects=True, vmem_limit_bytes=107 * 2**19
        ),
        name="sum_and_factor",
    )(panel, following)


def apply_kernel(root_rows, sums_ref, wide_ref, panel_ref, basis_ref, upper_ref, proj_ref):
    stacked = write_upper(root_rows, wide_ref, upper_ref)
    for block in range(sums_ref.shape[0] // panel_ref.shape[0]):
        write_projection(root_rows, stacked, sums_ref, proj_ref, block)
    write_basis(root_rows, stacked, panel_ref, basis_ref)


def applied(sums, wide, panel, next_count, root_rows):
    width, cells = panel.shape
    f32 = jnp.float32
    return pl.pallas_call(
        functools.partial(apply_kernel, root_rows),
        out_shape=(
            jax.ShapeDtypeStruct((width, cells), f32),
            jax.ShapeDtypeStruct((width, width), f32),
            jax.ShapeDtypeStruct((width, next_count), f32),
        ),
        compiler_params=pltpu.CompilerParams(vmem_limit_bytes=16 * 2**20),
        name="apply_factor",
    )(sums, wide, panel)


def plain_sums(panel, following):
    precise = functools.partial(
        lax.dot_general,
        dimension_numbers=(((1,), (1,)), ((), ())),
        precision=lax.Precision.HIGHEST,
        preferred_element_type=jnp.float32,
    )
    width = panel.shape[0]
    cross = lax.psum(
        jnp.concatenate([precise(panel, following), precise(panel, panel)], axis=1), ("gx", "gy")
    )
    blocks = cross.shape[1] // LANES
    sums = cross.reshape(width, blocks, LANES).transpose(1, 0, 2).reshape(blocks * width, LANES)
    wide = pl.pallas_call(
        lambda gram_ref, wide_ref: eliminate(gram_ref[...], wide_ref),
        out_shape=jax.ShapeDtypeStruct((width, 2 * width), jnp.float32),
        name="factor",
    )(cross[:, -width:])
    return sums, wide


def body(n_gx, n_gy, panel, following):
    width, cells = panel.shape
    root_rows = math.sqrt(cells * n_gx * n_gy)
    half_rows = (width + following.shape[0]) // LANES * width // 2
    if half_rows % (8 * (n_gx * n_gy // 2)) == 0:
        sums, wide = exchanged(panel, following, n_gx, n_gy)
    else:
        sums, wide = plain_sums(panel, following)
    return applied(sums, wide, panel, following.shape[0], root_rows)


def solution(mesh):
    return jax.shard_map(
        functools.partial(body, mesh.shape["gx"], mesh.shape["gy"]),
        mesh=mesh,
        in_specs=(P(None, ("gx", "gy")), P(None, ("gx", "gy"))),
        out_specs=(P(None, ("gx", "gy")), P(), P()),
        check_vma=False,
    )
```
